128 devices in a mesh: rows: 32 (over z, y, core), col: 4 (over x).
Axes of the slice: x: 4, y: 4, z: 4, core: 2. Of those that a mesh axis runs over, the one named last changes fastest.
Arguments:
- blocks: bfloat16 [4096, 16, 128, 128], P('rows', 'col')
- block_slot: int32 [4096, 16], P('rows', 'col'), may hold values from 0 to 399, as said below
- fetch_rows: int32 [128, 128, 2], P(('rows', 'col')), may hold values from 0 to 31
- basis: bfloat16 [4096, 128, 128], P(('rows', 'col')), may hold values from -15 to 15
Outputs:
- new_basis: float32 [4096, 128, 128], P(('rows', 'col'))
- factor: float32 [128, 128], replicated
The draws below stay inside these ranges and needn't reach their ends.
Inputs may be any that keep to these rules, and one draw needn't show every extreme that they name: `block_slot`: in positions c * 4 to c * 4 + 1 of each block row, values are below 144 and name a block row of the whole matrix; the other positions hold 144 or more. Position 0 of block row i names block row i.
All inputs are finite; a program needn't handle non-finite values.
Results may differ from the reference program's by a relative error of at most 0.0003.
Values may be sent and summed in bfloat16 or wider, within the bound.
A program may use at most 128 MiB of HBM per device.

```python
import jax
import jax.numpy as jnp
from jax import lax

B = 128
K = 128
BR_DEV = 128
NZ_DEV = 4
BAND_DEV = 2
HB = 8
SLOTS = 2
NBR = 4096
BQ_DEV = 32
N_ROWS = 32
N_COL = 4


def draw_blocks(key, part):
    key = jax.random.fold_in(key, 5)
    nbr = BR_DEV * N_ROWS
    nz = NZ_DEV * N_COL
    first, second = jax.random.split(key)
    place = jnp.arange(nbr, dtype=jnp.float32) / (nbr - 1)
    spread = jnp.exp(jnp.log(10.0) * jax.random.uniform(second, (nbr,), jnp.float32))
    entries = jnp.clip(jax.random.normal(first, (nbr, nz, B, B), jnp.float32), -6.0, 6.0)
    ramp = 1.0 + 2.0 * place
    scale = ramp * spread / jnp.sqrt(jnp.float32(nz * B))
    return (entries * scale[:, None, None, None]).astype(jnp.bfloat16)


def draw_block_slot(key, part):
    key = jax.random.fold_in(key, 11)
    nbr = BR_DEV * N_ROWS
    nz = NZ_DEV * N_COL
    span = BR_DEV + 2 * HB
    first, second = jax.random.split(key)
    rows = jnp.arange(nbr, dtype=jnp.int32)[:, None]
    slots = jnp.arange(nz, dtype=jnp.int32)[None, :]
    offset = jax.random.randint(first, (nbr, nz), -HB, HB + 1)
    offset = jnp.where(slots == 0, 0, offset)
    start = rows // BR_DEV * BR_DEV
    target = jnp.clip(rows + offset, 0, nbr - 1)
    band = target - start + HB
    far = span + jax.random.randint(second, (nbr, nz), 0, N_ROWS * N_COL * SLOTS)
    value = jnp.where(slots % NZ_DEV < BAND_DEV, band, far)
    value = value.at[0, nz - 1].set(span + N_ROWS * N_COL * SLOTS - 1)
    value = value.at[BR_DEV, 1].set(0)
    return value.astype(jnp.int32)


def draw_basis(key, part):
    key = jax.random.fold_in(key, 7)
    nbr = BR_DEV * N_ROWS
    first, second = jax.random.split(key, 2)
    column = jnp.exp(jnp.log(10.0) * jax.random.uniform(second, (K,), jnp.float32))
    value = jnp.clip(jax.random.normal(first, (nbr, B, K), jnp.float32), -6.0, 6.0) * column
    return (value / 4.0).astype(jnp.bfloat16)


def touch_ends(array, key, low, top_value):
    index_at = [jax.random.randint(jax.random.fold_in(key, axis), (), 0, length) for axis, length in enumerate(array.shape)]
    longest = array.shape.index(max(array.shape))
    neighbour = index_at[:longest] + [(index_at[longest] + 1) % array.shape[longest]] + index_at[longest + 1:]
    return array.at[tuple(index_at)].set(low).at[tuple(neighbour)].set(top_value)


def setup_inputs(seed: int = 0) -> dict:
    seeds = jax.random.split(jax.random.key(seed), 5)
    blocks = draw_blocks(jax.random.fold_in(seeds[4], 71), 0)
    block_slot = draw_block_slot(jax.random.fold_in(seeds[4], 71), 0)
    fetch_rows = touch_ends(jax.random.randint(seeds[2], (NBR // BQ_DEV, NBR // BQ_DEV, SLOTS), 0, BQ_DEV), jax.random.fold_in(seeds[2], 1), 0, BQ_DEV - 1).astype(jnp.int32)
    basis = draw_basis(jax.random.fold_in(seeds[4], 71), 0)
    return {"blocks": blocks, "block_slot": block_slot, "fetch_rows": fetch_rows, "basis": basis}


def reference(blocks, block_slot, fetch_rows, basis):
    nbr = blocks.shape[0]
    nz = blocks.shape[1]
    span = BR_DEV + 2 * HB
    peers = N_ROWS * N_COL
    rows = jnp.arange(nbr, dtype=jnp.int32)[:, None]
    slots = jnp.arange(nz, dtype=jnp.int32)[None, :]
    group = rows // BR_DEV
    requester = group * N_COL + slots // NZ_DEV
    band_col = group * BR_DEV - HB + block_slot
    flat = jnp.clip(block_slot - span, 0, peers * SLOTS - 1)
    owner = flat // SLOTS
    place = flat % SLOTS
    remote_col = owner * BQ_DEV + fetch_rows[requester, owner, place]
    column = jnp.where(block_slot < span, band_col, remote_col)
    column = jnp.clip(column, 0, nbr - 1).astype(jnp.int32)

    def one_group(pair):
        group_blocks, group_cols = pair
        picked = jnp.take(basis, group_cols, axis=0).astype(jnp.float32)
        return jnp.einsum('rsab,rsbk->rak', group_blocks.astype(jnp.float32), picked, precision=lax.Precision.HIGHEST)
    product = lax.map(one_group, (blocks.reshape((nbr // BR_DEV, BR_DEV) + blocks.shape[1:]), column.reshape(nbr // BR_DEV, BR_DEV, nz)))
    product = product.reshape(nbr * B, K)
    gram = lax.dot_general(product, product, (((0,), (0,)), ((), ())), precision=lax.Precision.HIGHEST)
    lower = jnp.linalg.cholesky(gram / (nbr * B))
    inverse = jax.scipy.linalg.solve_triangular(lower, jnp.eye(K, dtype=jnp.float32), lower=True).T
    new_basis = jnp.dot(product, inverse, precision=lax.Precision.HIGHEST)
    return (new_basis.reshape(nbr, B, K), lower.T)
```

```python
import functools

import jax
import jax.numpy as jnp
from jax import lax
from jax.experimental import pallas as pl
from jax.experimental.pallas import tpu as pltpu
from jax.sharding import PartitionSpec as P

HB = 8
BAND = 2
SLOTS = 2
ORDER = 11
FULL = 32767.0
F32 = jnp.float32
BF16 = jnp.bfloat16


def kernel(rows_n, cols_n, slot, fr, basis, blocks, part_out, gram_out,
           asks_v, asks_s, xb1, xb2, xb3, win, outb, fbuf, band_blk, far_blk, pband,
           sq, ss, rq, rs, gsrc, grecv, brecv, crecv,
           asem, hsem, xsend, xrecv, bsem, fsem, osend, frecv, qsend, qrecv, ssend, srecv,
           gsend, wsem):
    own = basis.shape[0]
    group = own * cols_n
    half = own // 2
    r = lax.axis_index("rows")
    c = lax.axis_index("col")
    MESH = pl.DeviceIdType.MESH

    def peer(k):
        o = lax.rem(k * ORDER, rows_n)
        oz, oy, oc = o // 8, lax.rem(o // 2, 4), lax.rem(o, 2)
        z, y, core = r // 8, lax.rem(r // 2, 4), lax.rem(r, 2)
        return (lax.rem(z + oz, 4) * 4 + lax.rem(y + oy, 4)) * 2 + lax.rem(core + oc, 2)

    def col_at(d):
        return lax.rem(c + d, cols_n)

    up = lax.rem(r + 1, rows_n)
    down = lax.rem(r + rows_n - 1, rows_n)

    def remote(src, dst, send, recv, row, col):
        return pltpu.make_async_remote_copy(
            src_ref=src, dst_ref=dst, send_sem=send, recv_sem=recv,
            device_id=(row, col), device_id_type=MESH)

    far_load = pltpu.make_async_copy(blocks.at[:, pl.ds(BAND, 2)], far_blk, bsem.at[2])
    far_load.start()

    def band_load(n):
        return pltpu.make_async_copy(
            blocks.at[pl.ds(n * 16, 16), pl.ds(0, BAND)], band_blk.at[lax.rem(n, 2)],
            bsem.at[lax.rem(n, 2)])

    band_load(0).start()
    band_load(1).start()

    barrier = pltpu.get_barrier_semaphore()

    def greet(k, _):
        pl.semaphore_signal(barrier, inc=1, device_id=(peer(k), c), device_id_type=MESH)
        return 0

    lax.fori_loop(1, rows_n, greet, 0)
    for d in range(1, cols_n):
        for row in (r, up, down):
            pl.semaphore_signal(barrier, inc=1, device_id=(row, col_at(d)), device_id_type=MESH)
    pl.semaphore_wait(barrier, rows_n - 1 + 3 * (cols_n - 1))

    def ask(k, _):
        p = peer(k)
        remote(fr.at[p], asks_v.at[r], asem.at[0], asem.at[1], p, c).start()
        return 0

    lax.fori_loop(1, rows_n, ask, 0)
    asks_v[pl.ds(r, 1)] = fr[pl.ds(r, 1)]

    x1 = remote(basis, xb3, xsend.at[0], xrecv.at[2], r, col_at(1))
    x3 = remote(basis, xb1, xsend.at[2], xrecv.at[0], r, col_at(3))
    x2 = remote(basis, xb2, xsend.at[1], xrecv.at[1], r, col_at(2))
    x1.start()
    x3.start()

    def halo(first, at, row, recv):
        return [
            remote(basis.at[pl.ds(first, HB)], win.at[pl.ds(at, HB)], hsem.at[d], recv, row, d)
            for d in range(cols_n)
        ]

    to_up = halo(own - HB, 0, up, hsem.at[cols_n])
    to_down = halo(0, HB + group, down, hsem.at[cols_n + 1])

    @pl.when(c == cols_n - 1)
    def _():
        for cp in to_up:
            cp.start()

    @pl.when(c == 0)
    def _():
        for cp in to_down:
            cp.start()

    def place(j, src):
        return pltpu.make_async_copy(
            src, win.at[pl.ds(HB + col_at(j) * own, own)], wsem.at[j])

    place(0, basis).start()

    every_ask = remote(asks_v.at[pl.ds(0, rows_n - 1)], asks_v.at[pl.ds(0, rows_n - 1)],
                       asem.at[0], asem.at[1], up, c)
    every_ask.wait_send()
    every_ask.wait_recv()
    to_scalar = pltpu.make_async_copy(asks_v, asks_s, asem.at[2])
    to_scalar.start()
    to_scalar.wait()

    def out_copy(k, j, n):
        p = peer(k)
        at = col_at(j) * SLOTS
        return remote(outb.at[pl.ds((n * rows_n + k) * SLOTS, SLOTS)],
                      fbuf.at[pl.ds(r * (cols_n * SLOTS) + at, SLOTS)],
                      osend.at[k], frecv, p, c)

    def serve(j, n, src, work=None):
        def step(k, _):
            p = peer(k)
            at = col_at(j) * SLOTS
            if work is not None:
                work(k)
            if n > 0:
                @pl.when(k > 0)
                def _():
                    out_copy(k, j, n - 1).wait_send()
            for q in range(SLOTS):
                row = jnp.clip(asks_s[p, 0, at + q], 0, own - 1)
                outb[(n * rows_n + k) * SLOTS + q] = src[row]

            @pl.when(k > 0)
            def _():
                out_copy(k, j, n).start()

            @pl.when(k == 0)
            def _():
                for q in range(SLOTS):
                    fbuf[r * (cols_n * SLOTS) + at + q] = outb[n * rows_n * SLOTS + q]
            return 0

        lax.fori_loop(0, rows_n, step, 0)

    serve(0, 0, basis)
    x1.wait_send()
    x3.wait_send()
    x2.start()
    x3.wait_recv()
    place(1, xb1).start()
    serve(1, 1, xb1)
    x1.wait_recv()
    place(3, xb3).start()
    serve(3, 2, xb3)
    x2.wait_recv()
    x2.wait_send()
    place(2, xb2).start()

    @pl.when(c == cols_n - 1)
    def _():
        for cp in to_up:
            cp.wait_send()

    @pl.when(c == 0)
    def _():
        for cp in to_down:
            cp.wait_send()

    to_up[0].wait_recv()
    to_down[0].wait_recv()
    for j, src in ((0, basis), (1, xb1), (2, xb2), (3, xb3)):
        place(j, src).wait()

    span = group + 2 * HB

    def multiply(left, first, second):
        a = jnp.concatenate([left[0], left[1]], axis=1)
        x = jnp.concatenate([first, second], axis=0)
        return jnp.dot(a, x, preferred_element_type=F32)

    def near(k):
        n = k // 4

        @pl.when(lax.rem(k, 4) == 0)
        def _():
            band_load(n).wait()

        for t in range(4):
            i = k * 4 + t
            v0 = jnp.clip(slot[i * 4], 0, span - 1)
            v1 = jnp.clip(slot[i * 4 + 1], 0, span - 1)
            pband[i] = multiply(band_blk[lax.rem(n, 2), lax.rem(k, 4) * 4 + t], win[v0], win[v1])

        @pl.when((lax.rem(k, 4) == 3) & (n < group // 16 - 2))
        def _():
            band_load(n + 2).start()

    serve(2, 3, xb2, near)

    def drain(k, _):
        out_copy(k, 2, 3).wait_send()
        return 0

    lax.fori_loop(1, rows_n, drain, 0)
    far_load.wait()
    remote(fbuf.at[pl.ds(0, (rows_n - 1) * cols_n * SLOTS)],
           fbuf.at[pl.ds(0, (rows_n - 1) * cols_n * SLOTS)],
           osend.at[0], frecv, up, c).wait_recv()

    limit = rows_n * cols_n * SLOTS - 1

    def whole(i):
        u0 = jnp.clip(slot[i * 4 + 2] - span, 0, limit)
        u1 = jnp.clip(slot[i * 4 + 3] - span, 0, limit)
        return pband[i] + multiply(far_blk[i], fbuf[u0], fbuf[u1])

    def plain(m, t):
        return rq[m, t].astype(jnp.int32).astype(F32) * rs[m, pl.ds(t, 1), :]

    def message(m, d, low, to, relay=None):
        first = col_at(d) * own + (0 if low else half)

        def step(t, _):
            total = whole(first + t)
            if relay is not None:
                total = total + plain(relay, t)
            top = jnp.maximum(jnp.max(jnp.abs(total), axis=0, keepdims=True), 1e-30)
            sq[m, t] = jnp.round(total * (FULL / top)).astype(jnp.int32).astype(jnp.int16)
            ss[m, pl.ds(t, 1), :] = top * (1.0 / FULL)
            return 0

        lax.fori_loop(0, half, step, 0, unroll=4)
        a = remote(sq.at[m], rq.at[m], qsend.at[m], qrecv.at[m], r, col_at(to))
        b = remote(ss.at[m], rs.at[m], ssend.at[m], srecv.at[m], r, col_at(to))
        a.start()
        b.start()
        return a, b

    def arrived(pair):
        pair[0].wait_recv()
        pair[1].wait_recv()

    m0 = message(0, 2, True, 1)
    m1 = message(1, 2, False, 3)
    m2 = message(2, 1, False, 1)
    m3 = message(3, 3, True, 3)

    mine = c * own

    def keep(t, _):
        part_out[t] = whole(mine + t)
        return 0

    lax.fori_loop(0, own, keep, 0, unroll=4)
    arrived(m0)
    m4 = message(4, 1, True, 1, relay=0)
    arrived(m1)
    m5 = message(5, 3, False, 3, relay=1)
    arrived(m2)
    arrived(m3)

    def early(t, _):
        part_out[t] = part_out[t] + plain(3, t)
        part_out[half + t] = part_out[half + t] + plain(2, t)
        return 0

    lax.fori_loop(0, half, early, 0, unroll=2)
    arrived(m4)
    arrived(m5)

    def gram_step(t, total):
        wide = []
        for at, m in ((t, 4), (half + t, 5)):
            p = part_out[at] + plain(m, t)
            part_out[at] = p
            high = p.astype(BF16)
            low = (p - high.astype(F32)).astype(BF16)
            wide.append(jnp.concatenate([high, low], axis=1))
        both = jnp.concatenate(wide, axis=0)
        return total + lax.dot_general(both, both, (((0,), (0,)), ((), ())),
                                       preferred_element_type=F32)

    size = basis.shape[2]
    total = lax.fori_loop(0, half, gram_step, jnp.zeros((2 * size, 2 * size), F32))
    gram = (total[:size, :size] + total[:size, size:]) + (total[size:, :size] + total[size:, size:])
    slab = size // 8
    gsrc[...] = gram.reshape(8, slab, size)

    core = lax.rem(r, 2)
    base = r - core
    me8 = c * 2 + core

    def eight(e):
        return (base + lax.rem(e, 2), e // 2)

    def pair8(d):
        e = lax.rem(me8 + d, 8)
        return e, eight(e)

    first = []
    for d in range(1, 8):
        e, (row, col) = pair8(d)
        cp = remote(gsrc.at[e], grecv.at[me8], gsend.at[0], gsend.at[1], row, col)
        cp.start()
        first.append(cp)
    grecv[pl.ds(me8, 1)] = gsrc[pl.ds(me8, 1)]
    all7 = remote(grecv.at[pl.ds(0, 7)], grecv.at[pl.ds(0, 7)], gsend.at[0], gsend.at[1], up, c)
    all7.wait_send()
    all7.wait_recv()
    part = grecv[0]
    for e in range(1, 8):
        part = part + grecv[e]
    spot = r // 2
    brecv[pl.ds(spot, 1)] = part[None]
    places = rows_n // 2
    for d in range(1, places):
        oz, oy = d // 4, d % 4
        z, y = r // 8, lax.rem(r // 2, 4)
        row = (lax.rem(z + oz, 4) * 4 + lax.rem(y + oy, 4)) * 2 + core
        remote(brecv.at[spot], brecv.at[spot], gsend.at[2], gsend.at[3], row, c).start()
    all15 = remote(brecv.at[pl.ds(0, places - 1)], brecv.at[pl.ds(0, places - 1)],
                   gsend.at[2], gsend.at[3], up, c)
    all15.wait_send()
    all15.wait_recv()
    part = brecv[0]
    for e in range(1, places):
        part = part + brecv[e]
    crecv[pl.ds(me8, 1)] = part[None]
    for d in range(1, 8):
        e, (row, col) = pair8(d)
        remote(crecv.at[me8], crecv.at[me8], gsend.at[4], gsend.at[5], row, col).start()
    back = remote(crecv.at[pl.ds(0, 7)], crecv.at[pl.ds(0, 7)], gsend.at[4], gsend.at[5], up, c)
    back.wait_send()
    back.wait_recv()
    gram_out[...] = crecv[...].reshape(size, size)
    for pair in (m0, m1, m2, m3, m4, m5):
        pair[0].wait_send()
        pair[1].wait_send()


def per_device(rows_n, cols_n, blocks, block_slot, fetch_rows, basis):
    own, size, rank = basis.shape
    group = own * cols_n
    half = own // 2
    per = cols_n * SLOTS
    span = group + 2 * HB
    requests = jnp.pad(fetch_rows.reshape(rows_n, 1, per), ((0, 0), (0, 0), (0, 128 - per)))
    vmem = pl.BlockSpec(memory_space=pltpu.VMEM)
    tile = (size, rank)
    dma = pltpu.SemaphoreType.DMA
    product, gram = pl.pallas_call(
        functools.partial(kernel, rows_n, cols_n),
        out_shape=(jax.ShapeDtypeStruct((own,) + tile, F32), jax.ShapeDtypeStruct((rank, rank), F32)),
        in_specs=[pl.BlockSpec(memory_space=pltpu.SMEM), vmem, vmem, pl.BlockSpec(memory_space=pl.ANY)],
        out_specs=(vmem, vmem),
        scratch_shapes=[
            pltpu.VMEM((rows_n, 1, 128), jnp.int32),
            pltpu.SMEM((rows_n, 1, 128), jnp.int32),
            pltpu.VMEM((own,) + tile, BF16),
            pltpu.VMEM((own,) + tile, BF16),
            pltpu.VMEM((own,) + tile, BF16),
            pltpu.VMEM((span,) + tile, BF16),
            pltpu.VMEM((rows_n * per,) + tile, BF16),
            pltpu.VMEM((rows_n * per,) + tile, BF16),
            pltpu.VMEM((2, 16, BAND, size, size), BF16),
            pltpu.VMEM((group, 2, size, size), BF16),
            pltpu.VMEM((group,) + tile, F32),
            pltpu.VMEM((6, half) + tile, jnp.int16),
            pltpu.VMEM((6, half, rank), F32),
            pltpu.VMEM((6, half) + tile, jnp.int16),
            pltpu.VMEM((6, half, rank), F32),
            pltpu.VMEM((8, rank // 8, rank), F32),
            pltpu.VMEM((8, rank // 8, rank), F32),
            pltpu.VMEM((rows_n // 2, rank // 8, rank), F32),
            pltpu.VMEM((8, rank // 8, rank), F32),
            dma((3,)),
            dma((cols_n + 2,)),
            dma((3,)),
            dma((3,)),
            dma((3,)),
            dma((1,)),
            dma((rows_n,)),
            dma,
            dma((6,)),
            dma((6,)),
            dma((6,)),
            dma((6,)),
            dma((6,)),
            dma((4,)),
        ],
        compiler_params=pltpu.CompilerParams(
            collective_id=0, has_side_effects=True, vmem_limit_bytes=62 * 2**20),
        name="product_and_gram",
    )(block_slot.reshape(-1), requests, basis, blocks)
    total_rows = rows_n * group * size
    lower = jnp.linalg.cholesky(gram / total_rows)
    inverse = jax.scipy.linalg.solve_triangular(
        lower, jnp.eye(rank, dtype=F32), lower=True
    ).T
    flat = product.reshape(-1, rank)
    result = jnp.dot(flat, inverse, precision=lax.Precision.HIGHEST).reshape(product.shape)
    return (result, lower.T)


def solution(mesh):
    in_specs = (
        P("rows", "col", None, None),
        P("rows", "col"),
        P(("rows", "col"), None, None),
        P(("rows", "col"), None, None),
    )
    out_specs = (P(("rows", "col"), None, None), P())
    step = functools.partial(per_device, mesh.shape["rows"], mesh.shape["col"])
    return jax.shard_map(
        step, mesh=mesh, in_specs=in_specs, out_specs=out_specs, check_vma=False
    )
```

```python
import functools

import jax
import jax.numpy as jnp
from jax import lax
from jax.experimental import pallas as pl
from jax.experimental.pallas import tpu as pltpu
from jax.sharding import PartitionSpec as P

HB = 8
BAND = 2
SLOTS = 2
ORDER = 11
FULL = 32767.0
PIVOT = 8
PART = 4
BATCHES = ((0, 0), (1, 0), (0, 1), (0, 3), (0, 2), (1, 1), (1, 3), (1, 2))
F32 = jnp.float32
BF16 = jnp.bfloat16


def kernel(rows_n, cols_n, slot, fr, basis, blocks, part_out, gram_out,
           asks_v, asks_s, xb1, xb2, xb3, win, outb, fbuf0, fbuf1, band_blk, far_blk, pband, pown,
           sq, ss, rq, rs, gsrc, grecv, brecv, crecv,
           asem, hsem, xsend, xrecv, bsem, fsem, osend, frecv, qsend, qrecv, ssend, srecv,
           gsend, wsem):
    own = basis.shape[0]
    group = own * cols_n
    r = lax.axis_index("rows")
    c = lax.axis_index("col")
    MESH = pl.DeviceIdType.MESH

    def peer(k):
        o = lax.rem(k * ORDER, rows_n)
        oz, oy, oc = o // 8, lax.rem(o // 2, 4), lax.rem(o, 2)
        z, y, core = r // 8, lax.rem(r // 2, 4), lax.rem(r, 2)
        return (lax.rem(z + oz, 4) * 4 + lax.rem(y + oy, 4)) * 2 + lax.rem(core + oc, 2)

    def col_at(d):
        return lax.rem(c + d, cols_n)

    up = lax.rem(r + 1, rows_n)
    down = lax.rem(r + rows_n - 1, rows_n)

    def remote(src, dst, send, recv, row, col):
        return pltpu.make_async_remote_copy(
            src_ref=src, dst_ref=dst, send_sem=send, recv_sem=recv,
            device_id=(row, col), device_id_type=MESH)

    far_load = pltpu.make_async_copy(blocks.at[:, pl.ds(BAND, 2)], far_blk, bsem.at[2])
    far_load.start()

    def band_load(n):
        return pltpu.make_async_copy(
            blocks.at[pl.ds(n * 16, 16), pl.ds(0, BAND)], band_blk.at[lax.rem(n, 2)],
            bsem.at[lax.rem(n, 2)])

    band_load(0).start()
    band_load(1).start()

    barrier = pltpu.get_barrier_semaphore()

    def greet(k, _):
        pl.semaphore_signal(barrier, inc=1, device_id=(peer(k), c), device_id_type=MESH)
        return 0

    lax.fori_loop(1, rows_n, greet, 0)
    for d in range(1, cols_n):
        for row in (r, up, down):
            pl.semaphore_signal(barrier, inc=1, device_id=(row, col_at(d)), device_id_type=MESH)
    pl.semaphore_wait(barrier, rows_n - 1 + 3 * (cols_n - 1))

    def ask(k, _):
        p = peer(k)
        remote(fr.at[p], asks_v.at[r], asem.at[0], asem.at[1], p, c).start()
        return 0

    lax.fori_loop(1, rows_n, ask, 0)
    asks_v[pl.ds(r, 1)] = fr[pl.ds(r, 1)]

    x1 = remote(basis, xb3, xsend.at[0], xrecv.at[2], r, col_at(1))
    x3 = remote(basis, xb1, xsend.at[2], xrecv.at[0], r, col_at(3))
    x2 = remote(basis, xb2, xsend.at[1], xrecv.at[1], r, col_at(2))
    x1.start()
    x3.start()

    def halo(first, at, row, recv):
        return [
            remote(basis.at[pl.ds(first, HB)], win.at[pl.ds(at, HB)], hsem.at[d], recv, row, d)
            for d in range(cols_n)
        ]

    to_up = halo(own - HB, 0, up, hsem.at[cols_n])
    to_down = halo(0, HB + group, down, hsem.at[cols_n + 1])

    @pl.when(c == cols_n - 1)
    def _():
        for cp in to_up:
            cp.start()

    @pl.when(c == 0)
    def _():
        for cp in to_down:
            cp.start()

    def place(j, src):
        return pltpu.make_async_copy(
            src, win.at[pl.ds(HB + col_at(j) * own, own)], wsem.at[j])

    place(0, basis).start()

    every_ask = remote(asks_v.at[pl.ds(0, rows_n - 1)], asks_v.at[pl.ds(0, rows_n - 1)],
                       asem.at[0], asem.at[1], up, c)
    every_ask.wait_send()
    every_ask.wait_recv()
    to_scalar = pltpu.make_async_copy(asks_v, asks_s, asem.at[2])
    to_scalar.start()
    to_scalar.wait()

    size = basis.shape[2]
    edge = size // 2
    lane = lax.broadcasted_iota(jnp.int32, (size, size), 1) < edge

    def swap(x):
        return pltpu.roll(x, edge, 1)

    fbuf = (fbuf0, fbuf1)

    def out_copy(k, h, j, n):
        p = peer(k)
        return remote(outb.at[n * rows_n + k], fbuf[h].at[r * cols_n + col_at(j)],
                      osend.at[k], frecv.at[h], p, c)

    def serve(n, work=None):
        h, j = BATCHES[n]
        src = (basis, xb1, xb2, xb3)[j]

        def step(k, _):
            p = peer(k)
            at = col_at(j) * SLOTS
            if work is not None:
                work(k)
            if n > 0:
                @pl.when(k > 0)
                def _():
                    out_copy(k, BATCHES[n - 1][0], BATCHES[n - 1][1], n - 1).wait_send()
            x0 = src[jnp.clip(asks_s[p, 0, at], 0, own - 1)]
            x1 = src[jnp.clip(asks_s[p, 0, at + 1], 0, own - 1)]
            if h == 0:
                both = jnp.concatenate([x0[:, :edge], x1[:, :edge]], axis=1)
            else:
                both = jnp.concatenate([x0[:, edge:], x1[:, edge:]], axis=1)
            outb[n * rows_n + k] = both

            @pl.when(k > 0)
            def _():
                out_copy(k, h, j, n).start()

            @pl.when(k == 0)
            def _():
                fbuf[h][r * cols_n + col_at(j)] = both
            return 0

        lax.fori_loop(0, rows_n, step, 0)

    serve(0)
    serve(1)
    x1.wait_send()
    x3.wait_send()
    x2.start()
    x3.wait_recv()
    place(1, xb1).start()
    serve(2)
    x1.wait_recv()
    place(3, xb3).start()
    serve(3)
    x2.wait_recv()
    x2.wait_send()
    place(2, xb2).start()

    @pl.when(c == cols_n - 1)
    def _():
        for cp in to_up:
            cp.wait_send()

    @pl.when(c == 0)
    def _():
        for cp in to_down:
            cp.wait_send()

    to_up[0].wait_recv()
    to_down[0].wait_recv()
    for j, src in ((0, basis), (1, xb1), (2, xb2), (3, xb3)):
        place(j, src).wait()

    span = group + 2 * HB

    def multiply(left, first, second):
        a = jnp.concatenate([left[0], left[1]], axis=1)
        x = jnp.concatenate([first, second], axis=0)
        return jnp.dot(a, x, preferred_element_type=F32)

    def near(k):
        n = k // 4

        @pl.when(lax.rem(k, 4) == 0)
        def _():
            band_load(n).wait()

        for t in range(2):
            b = []
            for e in range(2):
                i = k * 4 + t * 2 + e
                v0 = jnp.clip(slot[i * 4], 0, span - 1)
                v1 = jnp.clip(slot[i * 4 + 1], 0, span - 1)
                b.append(multiply(band_blk[lax.rem(n, 2), lax.rem(k, 4) * 4 + t * 2 + e], win[v0], win[v1]))
            pband[0, k * 2 + t] = jnp.where(lane, b[0], swap(b[1]))
            pband[1, k * 2 + t] = jnp.where(lane, swap(b[0]), b[1])

        @pl.when((lax.rem(k, 4) == 3) & (n < group // 16 - 2))
        def _():
            band_load(n + 2).start()

    serve(4, near)
    serve(5)
    far_load.wait()

    def fetched(h):
        count = (rows_n - 1) * cols_n
        remote(fbuf[h].at[pl.ds(0, count)], fbuf[h].at[pl.ds(0, count)],
               osend.at[0], frecv.at[h], up, c).wait_recv()

    limit = rows_n * cols_n * SLOTS - 1

    def whole(h, t):
        out = []
        for e in range(2):
            i = t * 2 + e
            x = []
            for q in range(2):
                u = jnp.clip(slot[i * 4 + 2 + q] - span, 0, limit)
                tile = fbuf[h][u // SLOTS]
                x.append(jnp.where(lax.rem(u, SLOTS) == e, tile, swap(tile)))
            out.append(multiply(far_blk[i], x[0], x[1]))
        return pband[h, t] + jnp.where(lane, out[0], out[1])

    def plain(h, m, t):
        return rq[h, m, t].astype(jnp.int32).astype(F32) * rs[h, m, t // PART, pl.ds(lax.rem(t, PART), 1), :]

    class Message:
        def __init__(self, h, m, d, low, to, relay=None):
            self.h, self.m, self.relay, self.to = h, m, relay, to
            self.first = col_at(d) * (own // 2) + (0 if low else quarter)

        def copies(self, part):
            h, m = self.h, self.m
            span_t = pl.ds(part * PART, PART)
            return (remote(sq.at[h, m, span_t], rq.at[h, m, span_t], qsend.at[h, m, part],
                           qrecv.at[h, m, part], r, col_at(self.to)),
                    remote(ss.at[h, m, part], rs.at[h, m, part], ssend.at[h, m, part],
                           srecv.at[h, m, part], r, col_at(self.to)))

        def tile(self, t):
            h, m = self.h, self.m
            total = whole(h, self.first + t)
            if self.relay is not None:
                total = total + plain(h, self.relay, t)
            top = jnp.maximum(jnp.max(jnp.abs(total), axis=0, keepdims=True), 1e-30)
            sq[h, m, t] = jnp.round(total * (FULL / top)).astype(jnp.int32).astype(jnp.int16)
            ss[h, m, t // PART, pl.ds(lax.rem(t, PART), 1), :] = top * (1.0 / FULL)

        def send(self, part):
            for cp in self.copies(part):
                cp.start()

        def arrived(self, part):
            for cp in self.copies(part):
                cp.wait_recv()

        def sent(self):
            for part in range(parts):
                for cp in self.copies(part):
                    cp.wait_send()

    quarter = own // 4
    parts = quarter // PART
    mine = c * (own // 2)

    def messages(h):
        return (Message(h, 0, 2, True, 1), Message(h, 1, 2, False, 3), Message(h, 2, 1, False, 1),
                Message(h, 3, 3, True, 3), Message(h, 4, 1, True, 1, relay=0),
                Message(h, 5, 3, False, 3, relay=1))

    def keep(h, t):
        pown[h, t] = whole(h, mine + t)

    def spread(group_of, k):
        for at, msg in enumerate(group_of):
            @pl.when(k // quarter == at)
            def _(msg=msg):
                t = lax.rem(k, quarter)
                if msg.relay is not None:
                    for part in range(parts):
                        @pl.when(t == part * PART)
                        def _(part=part):
                            early[msg.relay].arrived(part)
                msg.tile(t)
                for part in range(parts):
                    @pl.when(t == part * PART + PART - 1)
                    def _(part=part):
                        msg.send(part)

    early = messages(0)
    late = messages(1)
    fetched(0)
    serve(6, lambda k: spread(early[:4], k))

    def second(k):
        spread(early[4:], k)

        @pl.when(k >= 2 * quarter)
        def _():
            keep(0, k - 2 * quarter)

    serve(7, second)

    def add_own(h, pairs):
        def step(t, _):
            for m, high in pairs:
                at = quarter + t if high else t
                pown[h, at] = pown[h, at] + plain(h, m, t)
            return 0
        lax.fori_loop(0, quarter, step, 0, unroll=2)

    for m in range(2, 6):
        for part in range(parts):
            early[m].arrived(part)
    add_own(0, ((2, True), (3, False), (4, False), (5, True)))

    def drain(k, _):
        out_copy(k, BATCHES[7][0], BATCHES[7][1], 7).wait_send()
        return 0

    lax.fori_loop(1, rows_n, drain, 0)
    fetched(1)

    def run(msg):
        for part in range(parts):
            if msg.relay is not None:
                late[msg.relay].arrived(part)

            def step(t, _):
                msg.tile(part * PART + t)
                return 0
            lax.fori_loop(0, PART, step, 0, unroll=2)
            msg.send(part)

    for m in range(4):
        run(late[m])

    def keep_late(t, _):
        keep(1, t)
        return 0

    lax.fori_loop(0, own // 4, keep_late, 0, unroll=2)
    run(late[4])
    run(late[5])
    lax.fori_loop(own // 4, own // 2, keep_late, 0, unroll=2)
    for m in (2, 3):
        for part in range(parts):
            late[m].arrived(part)
    add_own(1, ((2, True), (3, False)))

    def gram_step(t, total):
        wide = []
        for at, m in ((t, 4), (quarter + t, 5)):
            first = pown[0, at]
            second = pown[1, at] + plain(1, m, t)
            for e, p in enumerate((jnp.where(lane, first, swap(second)),
                                   jnp.where(lane, swap(first), second))):
                high = p.astype(BF16)
                low = (p - high.astype(F32)).astype(BF16)
                wide.append(jnp.concatenate([high, low], axis=1))
                part_out[at * 2 + e] = wide[-1]
        both = jnp.concatenate(wide, axis=0)
        return total + lax.dot_general(both, both, (((0,), (0,)), ((), ())),
                                       preferred_element_type=F32)

    total = jnp.zeros((2 * size, 2 * size), F32)
    for part in range(parts):
        late[4].arrived(part)
        late[5].arrived(part)
        total = lax.fori_loop(part * PART, part * PART + PART, gram_step, total)
    gram = (total[:size, :size] + total[:size, size:]) + (total[size:, :size] + total[size:, size:])
    slab = size // 8
    gsrc[...] = gram.reshape(8, slab, size)

    core = lax.rem(r, 2)
    base = r - core
    me8 = c * 2 + core

    def eight(e):
        return (base + lax.rem(e, 2), e // 2)

    def pair8(d):
        e = lax.rem(me8 + d, 8)
        return e, eight(e)

    first = []
    for d in range(1, 8):
        e, (row, col) = pair8(d)
        cp = remote(gsrc.at[e], grecv.at[me8], gsend.at[0], gsend.at[1], row, col)
        cp.start()
        first.append(cp)
    grecv[pl.ds(me8, 1)] = gsrc[pl.ds(me8, 1)]
    all7 = remote(grecv.at[pl.ds(0, 7)], grecv.at[pl.ds(0, 7)], gsend.at[0], gsend.at[1], up, c)
    all7.wait_send()
    all7.wait_recv()
    part = grecv[0]
    for e in range(1, 8):
        part = part + grecv[e]
    spot = r // 2
    brecv[pl.ds(spot, 1)] = part[None]
    places = rows_n // 2
    for d in range(1, places):
        oz, oy = d // 4, d % 4
        z, y = r // 8, lax.rem(r // 2, 4)
        row = (lax.rem(z + oz, 4) * 4 + lax.rem(y + oy, 4)) * 2 + core
        remote(brecv.at[spot], brecv.at[spot], gsend.at[2], gsend.at[3], row, c).start()
    all15 = remote(brecv.at[pl.ds(0, places - 1)], brecv.at[pl.ds(0, places - 1)],
                   gsend.at[2], gsend.at[3], up, c)
    all15.wait_send()
    all15.wait_recv()
    part = brecv[0]
    for e in range(1, places):
        part = part + brecv[e]
    crecv[pl.ds(me8, 1)] = part[None]
    for d in range(1, 8):
        e, (row, col) = pair8(d)
        remote(crecv.at[me8], crecv.at[me8], gsend.at[4], gsend.at[5], row, col).start()
    back = remote(crecv.at[pl.ds(0, 7)], crecv.at[pl.ds(0, 7)], gsend.at[4], gsend.at[5], up, c)
    back.wait_send()
    back.wait_recv()
    gram_out[...] = crecv[...].reshape(size, size)
    for msg in early + late:
        msg.sent()


def factorize(gram):
    size = gram.shape[0]
    rows = [gram[8 * i:8 * i + 8, :] for i in range(size // 8)]
    upper = list(rows)
    lane = lax.broadcasted_iota(jnp.int32, (8, size), 1)
    sub = lax.broadcasted_iota(jnp.int32, (8, size), 0)

    def splat(v, k):
        return jnp.broadcast_to(v[:, k:k + 1], (8, size))

    for k in range(0, size, PIVOT):
        vi, s = k // 8, k % 8
        piece = rows[vi]
        r = [jnp.broadcast_to(piece[s + q:s + q + 1, :], (8, size)) for q in range(PIVOT)]
        a = [[splat(r[p], k + q) for q in range(p, PIVOT)] for p in range(PIVOT)]
        low = [[None] * PIVOT for _ in range(PIVOT)]
        inv = [None] * PIVOT
        for q in range(PIVOT):
            d = a[q][0]
            for m in range(q):
                d = d - low[q][m] * low[q][m]
            y = lax.rsqrt(d)
            inv[q] = y * (1.5 - (0.5 * d * y) * y)
            for p in range(q + 1, PIVOT):
                t = a[q][p - q]
                for m in range(q):
                    t = t - low[p][m] * low[q][m]
                low[p][q] = t * inv[q]
        w = [[None] * PIVOT for _ in range(PIVOT)]
        for q in range(PIVOT):
            w[q][q] = inv[q]
            for p in range(q + 1, PIVOT):
                t = low[p][q] * w[q][q]
                for m in range(q + 1, p):
                    t = t + low[p][m] * w[m][q]
                w[p][q] = -t * inv[p]
        block = (lane >= k) & (lane < k + PIVOT)
        rt = [jnp.where(block, jnp.where(lane == k + q, 1.0, 0.0), r[q]) for q in range(PIVOT)]
        scaled, factor = [], []
        for p in range(PIVOT):
            t, f = w[p][0] * rt[0], w[p][0] * r[0]
            for q in range(1, p + 1):
                t = t + w[p][q] * rt[q]
                f = f + w[p][q] * r[q]
            scaled.append(t)
            factor.append(f)
        back = []
        for q in range(PIVOT):
            t = w[q][q] * scaled[q]
            for p in range(q + 1, PIVOT):
                t = t + w[p][q] * scaled[p]
            back.append(t)
        for i in range(vi, size // 8):
            if i == vi and s + PIVOT == 8:
                new = rows[i]
            else:
                new = jnp.where(block, 0.0, rows[i])
                for q in range(PIVOT):
                    new = new - splat(rows[i], k + q) * back[q]
                if i == vi:
                    new = jnp.where(sub >= s + PIVOT, new, rows[i])
            if i == vi:
                up = upper[i] if s else jnp.zeros((8, size), F32)
                for p in range(PIVOT):
                    new = jnp.where((sub == s + p) & (lane <= k + p), scaled[p], new)
                    new = jnp.where((sub == s + p) & (lane > k + p), 0.0, new)
                    up = jnp.where((sub == s + p) & (lane >= k + p), factor[p], up)
                upper[i] = up
            rows[i] = new
    return jnp.concatenate(upper, axis=0), jnp.concatenate(rows, axis=0)


def orthonormalize(scale, gram, product, result, factor, weights):
    rank = gram.shape[0]

    @pl.when(pl.program_id(0) == 0)
    def _():
        upper, inverse = factorize(gram[...] * scale)
        factor[...] = upper
        turned = inverse.T
        high = turned.astype(BF16)
        low = (turned - high.astype(F32)).astype(BF16)
        both = jnp.concatenate([high, low], axis=1)
        weights[...] = jnp.concatenate([both, both], axis=0)

    wide = jnp.dot(product[...].reshape(-1, 2 * rank), weights[...], preferred_element_type=F32)
    result[...] = (wide[:, :rank] + wide[:, rank:]).reshape(result.shape)


def per_device(rows_n, cols_n, blocks, block_slot, fetch_rows, basis):
    own, size, rank = basis.shape
    group = own * cols_n
    quarter = own // 4
    parts = quarter // PART
    per = cols_n * SLOTS
    span = group + 2 * HB
    requests = jnp.pad(fetch_rows.reshape(rows_n, 1, per), ((0, 0), (0, 0), (0, 128 - per)))
    vmem = pl.BlockSpec(memory_space=pltpu.VMEM)
    tile = (size, rank)
    dma = pltpu.SemaphoreType.DMA
    product, gram = pl.pallas_call(
        functools.partial(kernel, rows_n, cols_n),
        out_shape=(jax.ShapeDtypeStruct((own, size, 2 * rank), BF16),
                   jax.ShapeDtypeStruct((rank, rank), F32)),
        in_specs=[pl.BlockSpec(memory_space=pltpu.SMEM), vmem, vmem, pl.BlockSpec(memory_space=pl.ANY)],
        out_specs=(vmem, vmem),
        scratch_shapes=[
            pltpu.VMEM((rows_n, 1, 128), jnp.int32),
            pltpu.SMEM((rows_n, 1, 128), jnp.int32),
            pltpu.VMEM((own,) + tile, BF16),
            pltpu.VMEM((own,) + tile, BF16),
            pltpu.VMEM((own,) + tile, BF16),
            pltpu.VMEM((span,) + tile, BF16),
            pltpu.VMEM((rows_n * per,) + tile, BF16),
            pltpu.VMEM((rows_n * cols_n,) + tile, BF16),
            pltpu.VMEM((rows_n * cols_n,) + tile, BF16),
            pltpu.VMEM((2, 16, BAND, size, size), BF16),
            pltpu.VMEM((group, 2, size, size), BF16),
            pltpu.VMEM((2, group // 2) + tile, F32),
            pltpu.VMEM((2, own // 2) + tile, F32),
            pltpu.VMEM((2, 6, quarter) + tile, jnp.int16),
            pltpu.VMEM((2, 6, parts, 8, rank), F32),
            pltpu.VMEM((2, 6, quarter) + tile, jnp.int16),
            pltpu.VMEM((2, 6, parts, 8, rank), F32),
            pltpu.VMEM((8, rank // 8, rank), F32),
            pltpu.VMEM((8, rank // 8, rank), F32),
            pltpu.VMEM((rows_n // 2, rank // 8, rank), F32),
            pltpu.VMEM((8, rank // 8, rank), F32),
            dma((3,)),
            dma((cols_n + 2,)),
            dma((3,)),
            dma((3,)),
            dma((3,)),
            dma((1,)),
            dma((rows_n,)),
            dma((2,)),
            dma((2, 6, parts)),
            dma((2, 6, parts)),
            dma((2, 6, parts)),
            dma((2, 6, parts)),
            dma((6,)),
            dma((4,)),
        ],
        compiler_params=pltpu.CompilerParams(
            collective_id=0, has_side_effects=True, vmem_limit_bytes=62 * 2**20),
        name="product_and_gram",
    )(block_slot.reshape(-1), requests, basis, blocks)
    total_rows = rows_n * group * size
    steps = 4
    at_once = own // steps
    return tuple(pl.pallas_call(
        functools.partial(orthonormalize, 1.0 / total_rows),
        out_shape=(jax.ShapeDtypeStruct((own,) + tile, F32),
                   jax.ShapeDtypeStruct((rank, rank), F32)),
        grid=(steps,),
        in_specs=[pl.BlockSpec((rank, rank), lambda n: (0, 0)),
                  pl.BlockSpec((at_once, size, 2 * rank), lambda n: (n, 0, 0))],
        out_specs=(pl.BlockSpec((at_once,) + tile, lambda n: (n, 0, 0)),
                   pl.BlockSpec((rank, rank), lambda n: (0, 0))),
        scratch_shapes=[pltpu.VMEM((2 * rank, 2 * rank), BF16)],
        name="orthonormalize",
    )(gram, product))


def solution(mesh):
    in_specs = (
        P("rows", "col", None, None),
        P("rows", "col"),
        P(("rows", "col"), None, None),
        P(("rows", "col"), None, None),
    )
    out_specs = (P(("rows", "col"), None, None), P())
    step = functools.partial(per_device, mesh.shape["rows"], mesh.shape["col"])
    return jax.shard_map(
        step, mesh=mesh, in_specs=in_specs, out_specs=out_specs, check_vma=False
    )
```

```python
import functools

import jax
import jax.numpy as jnp
from jax import lax
from jax.experimental import pallas as pl
from jax.experimental.pallas import tpu as pltpu
from jax.sharding import PartitionSpec as P

HB = 8
BAND = 2
SLOTS = 2
FULL = 32767.0
PIVOT = 8
PART = 4
BATCHES = ((0, 0), (1, 0), (0, 1), (0, 3), (0, 2), (1, 1), (1, 3), (1, 2))
F32 = jnp.float32
BF16 = jnp.bfloat16


def kernel(rows_n, cols_n, slot, fr, basis, blocks, part_out, gram_out,
           asks_v, asks_s, xb1, xb2, xb3, win, outb, fbuf0, fbuf1, band_blk, far_blk, pband, pown,
           sq, ss, rq, rs, gsrc, grecv, brecv, crecv,
           asem, hsem, xsend, xrecv, bsem, fsem, osend, frecv, qsend, qrecv, ssend, srecv,
           gsend, wsem):
    own = basis.shape[0]
    group = own * cols_n
    r = lax.axis_index("rows")
    c = lax.axis_index("col")
    MESH = pl.DeviceIdType.MESH

    def peer(k):
        e = k // 8
        first = 1 - (e + 3) // 4
        turn, oc = lax.rem(k, 4), lax.rem(k // 4, 2)
        cos = (1 - turn) * (1 - lax.rem(turn, 2))
        sin = (2 - turn) * lax.rem(turn, 2)
        y0, z0 = 1 + (3 - e) // 2, (4 - e) // 2
        turned_y, turned_z = cos * y0 - sin * z0, sin * y0 + cos * z0
        flat_y, flat_z = 2 * lax.rem(k // 2, 2), 2 * lax.rem(k // 4, 2)
        oy = first * flat_y + (1 - first) * turned_y
        oz = first * flat_z + (1 - first) * turned_z
        oc = first * lax.rem(k, 2) + (1 - first) * oc
        z, y, core = r // 8, lax.rem(r // 2, 4), lax.rem(r, 2)
        return (lax.rem(z + oz + 4, 4) * 4 + lax.rem(y + oy + 4, 4)) * 2 + lax.rem(core + oc, 2)

    def col_at(d):
        return lax.rem(c + d, cols_n)

    up = lax.rem(r + 1, rows_n)
    down = lax.rem(r + rows_n - 1, rows_n)

    def remote(src, dst, send, recv, row, col):
        return pltpu.make_async_remote_copy(
            src_ref=src, dst_ref=dst, send_sem=send, recv_sem=recv,
            device_id=(row, col), device_id_type=MESH)

    far_load = pltpu.make_async_copy(blocks.at[:, pl.ds(BAND, 2)], far_blk, bsem.at[2])
    far_load.start()

    def band_load(n):
        return pltpu.make_async_copy(
            blocks.at[pl.ds(n * 16, 16), pl.ds(0, BAND)], band_blk.at[lax.rem(n, 2)],
            bsem.at[lax.rem(n, 2)])

    band_load(0).start()
    band_load(1).start()

    barrier = pltpu.get_barrier_semaphore()

    def greet(k, _):
        pl.semaphore_signal(barrier, inc=1, device_id=(peer(k), c), device_id_type=MESH)
        return 0

    lax.fori_loop(1, rows_n, greet, 0)
    beside = r + 1 - 2 * lax.rem(r, 2)
    for d in range(1, cols_n):
        for row in (r, beside):
            pl.semaphore_signal(barrier, inc=1, device_id=(row, col_at(d)), device_id_type=MESH)
    pl.semaphore_wait(barrier, rows_n - 1 + 2 * (cols_n - 1))

    def ask(k, _):
        p = peer(k)
        remote(fr, asks_v.at[r], asem.at[0], asem.at[1], p, c).start()
        return 0

    lax.fori_loop(1, rows_n, ask, 0)
    asks_v[pl.ds(r, 1)] = fr[...].reshape((1,) + fr.shape)

    x1 = remote(basis, xb3, xsend.at[0], xrecv.at[2], r, col_at(1))
    x3 = remote(basis, xb1, xsend.at[2], xrecv.at[0], r, col_at(3))
    low, high = pl.ds(0, own // 2), pl.ds(own // 2, own // 2)
    x2a = remote(xb1.at[low], xb2.at[low], xsend.at[1], xrecv.at[1], r, col_at(3))
    x2b = remote(xb3.at[high], xb2.at[high], xsend.at[3], xrecv.at[3], r, col_at(1))
    x1.start()
    x3.start()

    def place(j, src):
        return pltpu.make_async_copy(
            src, win.at[pl.ds(HB + col_at(j) * own, own)], wsem.at[j])

    place(0, basis).start()

    size = basis.shape[2]
    edge = size // 2
    lane = lax.broadcasted_iota(jnp.int32, (size, size), 1) < edge

    def swap(x):
        return pltpu.roll(x, edge, 1)

    fbuf = (fbuf0, fbuf1)

    def out_copy(k, h, j, n):
        p = peer(k)
        return remote(outb.at[n * rows_n + k], fbuf[h].at[r * cols_n + col_at(j)],
                      osend.at[k], frecv.at[h], p, c)

    def serve(n, work=None):
        h, j = BATCHES[n]
        src = (basis, xb1, xb2, xb3)[j]

        def step(k, _):
            p = peer(k)
            at = r * cols_n + col_at(j)
            if work is not None:
                work(k)
            if n > 0:
                @pl.when(k > 0)
                def _():
                    out_copy(k, BATCHES[n - 1][0], BATCHES[n - 1][1], n - 1).wait_send()
            x0 = src[jnp.clip(asks_s[p, 0, at], 0, own - 1)]
            x1 = src[jnp.clip(asks_s[p, 1, at], 0, own - 1)]
            if h == 0:
                both = jnp.concatenate([x0[:, :edge], x1[:, :edge]], axis=1)
            else:
                both = jnp.concatenate([x0[:, edge:], x1[:, edge:]], axis=1)
            outb[n * rows_n + k] = both

            @pl.when(k > 0)
            def _():
                out_copy(k, h, j, n).start()

            @pl.when(k == 0)
            def _():
                fbuf[h][r * cols_n + col_at(j)] = both
            return 0

        lax.fori_loop(0, rows_n, step, 0)

    every_ask = remote(asks_v.at[pl.ds(0, rows_n - 1)], asks_v.at[pl.ds(0, rows_n - 1)],
                       asem.at[0], asem.at[1], up, c)
    every_ask.wait_send()
    every_ask.wait_recv()
    to_scalar = pltpu.make_async_copy(asks_v, asks_s, asem.at[2])
    to_scalar.start()
    to_scalar.wait()
    serve(0)
    serve(1)
    x3.wait_recv()
    x2a.start()
    x1.wait_recv()
    x2b.start()
    place(1, xb1).start()
    place(3, xb3).start()
    serve(2)
    serve(3)
    x2a.wait_recv()
    x2b.wait_recv()
    place(2, xb2).start()
    for j, src in ((0, basis), (1, xb1), (3, xb3), (2, xb2)):
        place(j, src).wait()

    to_up = remote(win.at[pl.ds(group, HB)], win.at[pl.ds(0, HB)], hsem.at[0], hsem.at[1], up, c)
    to_down = remote(win.at[pl.ds(HB, HB)], win.at[pl.ds(HB + group, HB)], hsem.at[2], hsem.at[3], down, c)
    to_up.start()
    to_down.start()

    span = group + 2 * HB

    def multiply(left, first, second):
        a = jnp.concatenate([left[0], left[1]], axis=1)
        x = jnp.concatenate([first, second], axis=0)
        return jnp.dot(a, x, preferred_element_type=F32)

    def near(k):
        n = k // 4

        @pl.when(lax.rem(k, 4) == 0)
        def _():
            band_load(n).wait()

        for t in range(2):
            b = []
            for e in range(2):
                i = k * 4 + t * 2 + e
                v0 = jnp.clip(slot[0, i], 0, span - 1)
                v1 = jnp.clip(slot[1, i], 0, span - 1)
                b.append(multiply(band_blk[lax.rem(n, 2), lax.rem(k, 4) * 4 + t * 2 + e], win[v0], win[v1]))
            pband[0, k * 2 + t] = jnp.where(lane, b[0], swap(b[1]))
            pband[1, k * 2 + t] = jnp.where(lane, swap(b[0]), b[1])

        @pl.when((lax.rem(k, 4) == 3) & (n < group // 16 - 2))
        def _():
            band_load(n + 2).start()

    serve(4)
    to_up.wait()
    to_down.wait()
    x1.wait_send()
    x3.wait_send()
    x2a.wait_send()
    x2b.wait_send()
    serve(5, near)
    far_load.wait()

    def fetched(h):
        count = (rows_n - 1) * cols_n
        remote(fbuf[h].at[pl.ds(0, count)], fbuf[h].at[pl.ds(0, count)],
               osend.at[0], frecv.at[h], up, c).wait_recv()

    limit = rows_n * cols_n * SLOTS - 1

    def whole(h, t):
        out = []
        for e in range(2):
            i = t * 2 + e
            x = []
            for q in range(2):
                u = jnp.clip(slot[2 + q, i] - span, 0, limit)
                tile = fbuf[h][u // SLOTS]
                x.append(jnp.where(lax.rem(u, SLOTS) == e, tile, swap(tile)))
            out.append(multiply(far_blk[i], x[0], x[1]))
        return pband[h, t] + jnp.where(lane, out[0], out[1])

    def plain(h, m, t):
        return rq[h, m, t].astype(jnp.int32).astype(F32) * rs[h, m, t // PART, pl.ds(lax.rem(t, PART), 1), :]

    class Message:
        def __init__(self, h, m, d, low, to, relay=None):
            self.h, self.m, self.relay, self.to = h, m, relay, to
            self.first = col_at(d) * (own // 2) + (0 if low else quarter)

        def copies(self, part):
            h, m = self.h, self.m
            span_t = pl.ds(part * PART, PART)
            return (remote(sq.at[h, m, span_t], rq.at[h, m, span_t], qsend.at[h, m, part],
                           qrecv.at[h, m, part], r, col_at(self.to)),
                    remote(ss.at[h, m, part], rs.at[h, m, part], ssend.at[h, m, part],
                           srecv.at[h, m, part], r, col_at(self.to)))

        def tile(self, t):
            h, m = self.h, self.m
            total = whole(h, self.first + t)
            if self.relay is not None:
                total = total + plain(h, self.relay, t)
            top = jnp.maximum(jnp.max(jnp.abs(total), axis=0, keepdims=True), 1e-30)
            sq[h, m, t] = jnp.round(total * (FULL / top)).astype(jnp.int32).astype(jnp.int16)
            ss[h, m, t // PART, pl.ds(lax.rem(t, PART), 1), :] = top * (1.0 / FULL)

        def send(self, part):
            for cp in self.copies(part):
                cp.start()

        def arrived(self, part):
            for cp in self.copies(part):
                cp.wait_recv()

        def sent(self):
            for part in range(parts):
                for cp in self.copies(part):
                    cp.wait_send()

    quarter = own // 4
    parts = quarter // PART
    mine = c * (own // 2)

    def messages(h):
        return (Message(h, 0, 2, True, 1), Message(h, 1, 2, False, 3), Message(h, 2, 1, False, 1),
                Message(h, 3, 3, True, 3), Message(h, 4, 1, True, 1, relay=0),
                Message(h, 5, 3, False, 3, relay=1))

    def keep(h, t):
        pown[h, t] = whole(h, mine + t)

    def spread(group_of, k):
        for at, msg in enumerate(group_of):
            @pl.when(k // quarter == at)
            def _(msg=msg):
                t = lax.rem(k, quarter)
                if msg.relay is not None:
                    for part in range(parts):
                        @pl.when(t == part * PART)
                        def _(part=part):
                            early[msg.relay].arrived(part)
                msg.tile(t)
                for part in range(parts):
                    @pl.when(t == part * PART + PART - 1)
                    def _(part=part):
                        msg.send(part)

    early = messages(0)
    late = messages(1)
    fetched(0)
    serve(6, lambda k: spread(early[:4], k))

    def second(k):
        spread(early[4:], k)

        @pl.when(k >= 2 * quarter)
        def _():
            keep(0, k - 2 * quarter)

    serve(7, second)

    def add_own(h, pairs):
        def step(t, _):
            for m, high in pairs:
                at = quarter + t if high else t
                pown[h, at] = pown[h, at] + plain(h, m, t)
            return 0
        lax.fori_loop(0, quarter, step, 0, unroll=2)

    for m in range(2, 6):
        for part in range(parts):
            early[m].arrived(part)
    add_own(0, ((2, True), (3, False), (4, False), (5, True)))

    def drain(k, _):
        out_copy(k, BATCHES[7][0], BATCHES[7][1], 7).wait_send()
        return 0

    lax.fori_loop(1, rows_n, drain, 0)
    fetched(1)

    def run(msg):
        for part in range(parts):
            if msg.relay is not None:
                late[msg.relay].arrived(part)

            def step(t, _):
                msg.tile(part * PART + t)
                return 0
            lax.fori_loop(0, PART, step, 0, unroll=2)
            msg.send(part)

    for m in range(4):
        run(late[m])

    def keep_late(t, _):
        keep(1, t)
        return 0

    lax.fori_loop(0, own // 4, keep_late, 0, unroll=2)
    run(late[4])
    run(late[5])
    lax.fori_loop(own // 4, own // 2, keep_late, 0, unroll=2)
    for m in (2, 3):
        for part in range(parts):
            late[m].arrived(part)
    add_own(1, ((2, True), (3, False)))

    def gram_step(t, total):
        wide = []
        for at, m in ((t, 4), (quarter + t, 5)):
            first = pown[0, at]
            second = pown[1, at] + plain(1, m, t)
            for e, p in enumerate((jnp.where(lane, first, swap(second)),
                                   jnp.where(lane, swap(first), second))):
                high = p.astype(BF16)
                low = (p - high.astype(F32)).astype(BF16)
                wide.append(jnp.concatenate([high, low], axis=1))
                part_out[at * 2 + e] = wide[-1]
        both = jnp.concatenate(wide, axis=0)
        return total + lax.dot_general(both, both, (((0,), (0,)), ((), ())),
                                       preferred_element_type=F32)

    total = jnp.zeros((2 * size, 2 * size), F32)
    for part in range(parts):
        late[4].arrived(part)
        late[5].arrived(part)
        total = lax.fori_loop(part * PART, part * PART + PART, gram_step, total)
    gram = (total[:size, :size] + total[:size, size:]) + (total[size:, :size] + total[size:, size:])
    slab = size // 8
    gsrc[...] = gram.reshape(8, slab, size)

    core = lax.rem(r, 2)
    base = r - core
    me8 = c * 2 + core

    def eight(e):
        return (base + lax.rem(e, 2), e // 2)

    def pair8(d):
        e = lax.rem(me8 + d, 8)
        return e, eight(e)

    first = []
    for d in range(1, 8):
        e, (row, col) = pair8(d)
        cp = remote(gsrc.at[e], grecv.at[me8], gsend.at[0], gsend.at[1], row, col)
        cp.start()
        first.append(cp)
    grecv[pl.ds(me8, 1)] = gsrc[pl.ds(me8, 1)]
    all7 = remote(grecv.at[pl.ds(0, 7)], grecv.at[pl.ds(0, 7)], gsend.at[0], gsend.at[1], up, c)
    all7.wait_send()
    all7.wait_recv()
    part = grecv[0]
    for e in range(1, 8):
        part = part + grecv[e]
    spot = r // 2
    brecv[pl.ds(spot, 1)] = part[None]
    places = rows_n // 2
    for d in (10, 11, 9, 6, 14, 2, 8, 5, 7, 13, 15, 1, 3, 4, 12):
        oz, oy = d // 4, d % 4
        z, y = r // 8, lax.rem(r // 2, 4)
        row = (lax.rem(z + oz, 4) * 4 + lax.rem(y + oy, 4)) * 2 + core
        remote(brecv.at[spot], brecv.at[spot], gsend.at[2], gsend.at[3], row, c).start()
    all15 = remote(brecv.at[pl.ds(0, places - 1)], brecv.at[pl.ds(0, places - 1)],
                   gsend.at[2], gsend.at[3], up, c)
    all15.wait_send()
    all15.wait_recv()
    part = brecv[0]
    for e in range(1, places):
        part = part + brecv[e]
    crecv[pl.ds(me8, 1)] = part[None]
    for d in range(1, 8):
        e, (row, col) = pair8(d)
        remote(crecv.at[me8], crecv.at[me8], gsend.at[4], gsend.at[5], row, col).start()
    back = remote(crecv.at[pl.ds(0, 7)], crecv.at[pl.ds(0, 7)], gsend.at[4], gsend.at[5], up, c)
    back.wait_send()
    back.wait_recv()
    gram_out[...] = crecv[...].reshape(size, size)
    for msg in early + late:
        msg.sent()


def factorize(gram):
    size = gram.shape[0]
    rows = [gram[8 * i:8 * i + 8, :] for i in range(size // 8)]
    upper = list(rows)
    lane = lax.broadcasted_iota(jnp.int32, (8, size), 1)
    sub = lax.broadcasted_iota(jnp.int32, (8, size), 0)

    def splat(v, k):
        return jnp.broadcast_to(v[:, k:k + 1], (8, size))

    for k in range(0, size, PIVOT):
        vi, s = k // 8, k % 8
        piece = rows[vi]
        r = [jnp.broadcast_to(piece[s + q:s + q + 1, :], (8, size)) for q in range(PIVOT)]
        a = [[splat(r[p], k + q) for q in range(p, PIVOT)] for p in range(PIVOT)]
        block = (lane >= k) & (lane < k + PIVOT)
        rt = [jnp.where(block, jnp.where(lane == k + q, 1.0, 0.0), r[q]) for q in range(PIVOT)]
        low = [[None] * PIVOT for _ in range(PIVOT)]
        inv, scaled, factor = [], [], []
        below = [i for i in range(vi, size // 8) if i > vi or s + PIVOT < 8]
        column = {i: [splat(rows[i], k + q) for q in range(PIVOT)] for i in below}
        new_rows = {i: jnp.where(block, 0.0, rows[i]) for i in below}
        for p in range(PIVOT):
            d = a[p][0]
            for m in range(p):
                d = d - low[p][m] * low[p][m]
            y = lax.rsqrt(d)
            inv.append(y * (1.5 - (0.5 * d * y) * y))
            t, f = rt[p], r[p]
            for m in range(p):
                t = t - low[p][m] * scaled[m]
                f = f - low[p][m] * factor[m]
            scaled.append(t * inv[p])
            factor.append(f * inv[p])
            for i in below:
                t = column[i][p]
                for m in range(p):
                    t = t - low[p][m] * column[i][m]
                column[i][p] = t * inv[p]
                new_rows[i] = new_rows[i] - column[i][p] * scaled[p]
            for n in range(p + 1, PIVOT):
                t = a[p][n - p]
                for m in range(p):
                    t = t - low[n][m] * low[p][m]
                low[n][p] = t * inv[p]
        for i in range(vi, size // 8):
            new = new_rows.get(i, rows[i])
            if i == vi and i in new_rows:
                new = jnp.where(sub >= s + PIVOT, new, rows[i])
            if i == vi:
                up = upper[i] if s else jnp.zeros((8, size), F32)
                for p in range(PIVOT):
                    new = jnp.where((sub == s + p) & (lane <= k + p), scaled[p], new)
                    new = jnp.where((sub == s + p) & (lane > k + p), 0.0, new)
                    up = jnp.where((sub == s + p) & (lane >= k + p), factor[p], up)
                upper[i] = up
            rows[i] = new
    return jnp.concatenate(upper, axis=0), jnp.concatenate(rows, axis=0)


def orthonormalize(scale, gram, product, result, factor, weights):
    rank = gram.shape[0]

    @pl.when(pl.program_id(0) == 0)
    def _():
        upper, inverse = factorize(gram[...] * scale)
        factor[...] = upper
        turned = inverse.T
        high = turned.astype(BF16)
        low = (turned - high.astype(F32)).astype(BF16)
        both = jnp.concatenate([high, low], axis=1)
        weights[...] = jnp.concatenate([both, both], axis=0)

    wide = jnp.dot(product[...].reshape(-1, 2 * rank), weights[...], preferred_element_type=F32)
    result[...] = (wide[:, :rank] + wide[:, rank:]).reshape(result.shape)


def per_device(rows_n, cols_n, blocks, block_slot, fetch_rows, basis):
    own, size, rank = basis.shape
    group = own * cols_n
    quarter = own // 4
    parts = quarter // PART
    per = cols_n * SLOTS
    span = group + 2 * HB
    vmem = pl.BlockSpec(memory_space=pltpu.VMEM)
    tile = (size, rank)
    dma = pltpu.SemaphoreType.DMA
    product, gram = pl.pallas_call(
        functools.partial(kernel, rows_n, cols_n),
        out_shape=(jax.ShapeDtypeStruct((own, size, 2 * rank), BF16),
                   jax.ShapeDtypeStruct((rank, rank), F32)),
        in_specs=[pl.BlockSpec(memory_space=pltpu.SMEM), vmem, vmem, pl.BlockSpec(memory_space=pl.ANY)],
        out_specs=(vmem, vmem),
        scratch_shapes=[
            pltpu.VMEM((rows_n, SLOTS, rows_n * cols_n), jnp.int32),
            pltpu.SMEM((rows_n, SLOTS, rows_n * cols_n), jnp.int32),
            pltpu.VMEM((own,) + tile, BF16),
            pltpu.VMEM((own,) + tile, BF16),
            pltpu.VMEM((own,) + tile, BF16),
            pltpu.VMEM((span,) + tile, BF16),
            pltpu.VMEM((rows_n * per,) + tile, BF16),
            pltpu.VMEM((rows_n * cols_n,) + tile, BF16),
            pltpu.VMEM((rows_n * cols_n,) + tile, BF16),
            pltpu.VMEM((2, 16, BAND, size, size), BF16),
            pltpu.VMEM((group, 2, size, size), BF16),
            pltpu.VMEM((2, group // 2) + tile, F32),
            pltpu.VMEM((2, own // 2) + tile, F32),
            pltpu.VMEM((2, 6, quarter) + tile, jnp.int16),
            pltpu.VMEM((2, 6, parts, 8, rank), F32),
            pltpu.VMEM((2, 6, quarter) + tile, jnp.int16),
            pltpu.VMEM((2, 6, parts, 8, rank), F32),
            pltpu.VMEM((8, rank // 8, rank), F32),
            pltpu.VMEM((8, rank // 8, rank), F32),
            pltpu.VMEM((rows_n // 2, rank // 8, rank), F32),
            pltpu.VMEM((8, rank // 8, rank), F32),
            dma((3,)),
            dma((4,)),
            dma((4,)),
            dma((4,)),
            dma((3,)),
            dma((1,)),
            dma((rows_n,)),
            dma((2,)),
            dma((2, 6, parts)),
            dma((2, 6, parts)),
            dma((2, 6, parts)),
            dma((2, 6, parts)),
            dma((6,)),
            dma((4,)),
        ],
        compiler_params=pltpu.CompilerParams(
            collective_id=0, has_side_effects=True, vmem_limit_bytes=62 * 2**20),
        name="product_and_gram",
    )(block_slot.T, fetch_rows[0].T, basis, blocks)
    total_rows = rows_n * group * size
    steps = 4
    at_once = own // steps
    return tuple(pl.pallas_call(
        functools.partial(orthonormalize, 1.0 / total_rows),
        out_shape=(jax.ShapeDtypeStruct((own,) + tile, F32),
                   jax.ShapeDtypeStruct((rank, rank), F32)),
        grid=(steps,),
        in_specs=[pl.BlockSpec((rank, rank), lambda n: (0, 0)),
                  pl.BlockSpec((at_once, size, 2 * rank), lambda n: (n, 0, 0))],
        out_specs=(pl.BlockSpec((at_once,) + tile, lambda n: (n, 0, 0)),
                   pl.BlockSpec((rank, rank), lambda n: (0, 0))),
        scratch_shapes=[pltpu.VMEM((2 * rank, 2 * rank), BF16)],
        name="orthonormalize",
    )(gram, product))


def solution(mesh):
    in_specs = (
        P("rows", "col", None, None),
        P("rows", "col"),
        P(("rows", "col"), None, None),
        P(("rows", "col"), None, None),
    )
    out_specs = (P(("rows", "col"), None, None), P())
    step = functools.partial(per_device, mesh.shape["rows"], mesh.shape["col"])
    return jax.shard_map(
        step, mesh=mesh, in_specs=in_specs, out_specs=out_specs, check_vma=False
    )
```

```python
import functools

import jax
import jax.numpy as jnp
from jax import lax
from jax.experimental import pallas as pl
from jax.experimental.pallas import tpu as pltpu
from jax.sharding import PartitionSpec as P

HB = 8
BAND = 2
SLOTS = 2
FULL = 32767.0
PIVOT = 8
PART = 8
CHUNKS = ((0, 64), (64, 32), (96, 32))
BATCHES = ((0, 0, 1), (1, 0, 1), (2, 0, 1), (0, 1, 1), (0, 3, 1), (0, 2, 1), (1, 1, 3), (2, 1, 3))
F32 = jnp.float32
BF16 = jnp.bfloat16


def kernel(rows_n, cols_n, slot, fr, basis, blocks, part_out, gram_out, *scratch):
    (asks_v, asks_s, basis_t, xb1, xb2, xb3, win, outs, fbufs, band_blk, far_blk, pband, pown,
     sqs, ss, rqs, rs, gsrc, grecv, brecv, crecv,
     asem, hsem, xsend, xrecv, bsem, osend, frecv, qsend, qrecv, ssend, srecv, gsend, wsem) = scratch
    own = basis.shape[0]
    group = own * cols_n
    r = lax.axis_index("rows")
    c = lax.axis_index("col")
    MESH = pl.DeviceIdType.MESH

    def peer(k):
        e = k // 8
        first = 1 - (e + 3) // 4
        turn, oc = lax.rem(k, 4), lax.rem(k // 4, 2)
        cos = (1 - turn) * (1 - lax.rem(turn, 2))
        sin = (2 - turn) * lax.rem(turn, 2)
        y0, z0 = 1 + (3 - e) // 2, (4 - e) // 2
        turned_y, turned_z = cos * y0 - sin * z0, sin * y0 + cos * z0
        flat_y, flat_z = 2 * lax.rem(k // 2, 2), 2 * lax.rem(k // 4, 2)
        oy = first * flat_y + (1 - first) * turned_y
        oz = first * flat_z + (1 - first) * turned_z
        oc = first * lax.rem(k, 2) + (1 - first) * oc
        z, y, core = r // 8, lax.rem(r // 2, 4), lax.rem(r, 2)
        return (lax.rem(z + oz + 4, 4) * 4 + lax.rem(y + oy + 4, 4)) * 2 + lax.rem(core + oc, 2)

    def col_at(d):
        return lax.rem(c + d, cols_n)

    up = lax.rem(r + 1, rows_n)
    down = lax.rem(r + rows_n - 1, rows_n)

    def remote(src, dst, send, recv, row, col):
        return pltpu.make_async_remote_copy(
            src_ref=src, dst_ref=dst, send_sem=send, recv_sem=recv,
            device_id=(row, col), device_id_type=MESH)

    far_load = pltpu.make_async_copy(blocks.at[:, pl.ds(BAND, 2)], far_blk, bsem.at[2])
    far_load.start()

    def band_load(n):
        return pltpu.make_async_copy(
            blocks.at[pl.ds(n * 16, 16), pl.ds(0, BAND)], band_blk.at[lax.rem(n, 2)],
            bsem.at[lax.rem(n, 2)])

    band_load(0).start()
    band_load(1).start()

    barrier = pltpu.get_barrier_semaphore()

    def greet(k, _):
        pl.semaphore_signal(barrier, inc=1, device_id=(peer(k), c), device_id_type=MESH)
        return 0

    lax.fori_loop(1, rows_n, greet, 0)
    beside = r + 1 - 2 * lax.rem(r, 2)
    for d in range(1, cols_n):
        for row in (r, beside):
            pl.semaphore_signal(barrier, inc=1, device_id=(row, col_at(d)), device_id_type=MESH)

    def turn(i, _):
        basis_t[i] = basis[i].T
        return 0

    lax.fori_loop(0, own, turn, 0, unroll=2)
    pl.semaphore_wait(barrier, rows_n - 1 + 2 * (cols_n - 1))

    def ask(k, _):
        p = peer(k)
        remote(fr, asks_v.at[r], asem.at[0], asem.at[1], p, c).start()
        return 0

    lax.fori_loop(1, rows_n, ask, 0)
    asks_v[pl.ds(r, 1)] = fr[...].reshape((1,) + fr.shape)

    x1 = remote(basis_t, xb3, xsend.at[0], xrecv.at[2], r, col_at(1))
    x3 = remote(basis_t, xb1, xsend.at[2], xrecv.at[0], r, col_at(3))
    low, high = pl.ds(0, own // 2), pl.ds(own // 2, own // 2)
    x2a = remote(xb1.at[low], xb2.at[low], xsend.at[1], xrecv.at[1], r, col_at(3))
    x2b = remote(xb3.at[high], xb2.at[high], xsend.at[3], xrecv.at[3], r, col_at(1))
    x1.start()
    x3.start()

    def place(j, src):
        return pltpu.make_async_copy(
            src, win.at[pl.ds(HB + col_at(j) * own, own)], wsem.at[j])

    place(0, basis_t).start()

    size = basis.shape[2]
    per = cols_n * SLOTS

    def out_copy(k, n):
        h, j, count = BATCHES[n]
        at = j * SLOTS
        return remote(outs[h].at[pl.ds(k * per + at, count * SLOTS)],
                      fbufs[h].at[pl.ds(r * per + at, count * SLOTS)],
                      osend.at[n % 2, k], frecv.at[h], peer(k), c)

    def serve(n):
        h, j0, count = BATCHES[n]
        first, width = CHUNKS[h]

        def step(k, _):
            p = peer(k)
            if n > 1:
                @pl.when(k > 0)
                def _():
                    out_copy(k, n - 2).wait_send()
            for j in range(j0, j0 + count):
                src = (basis_t, xb1, xb2, xb3)[j]
                at = r * cols_n + col_at(j)
                for q in range(SLOTS):
                    row = jnp.clip(asks_s[p, q, at], 0, own - 1)
                    outs[h][k * per + j * SLOTS + q] = src[row, first:first + width, :]

            @pl.when(k > 0)
            def _():
                out_copy(k, n).start()

            @pl.when(k == 0)
            def _():
                for t in range(j0 * SLOTS, (j0 + count) * SLOTS):
                    fbufs[h][r * per + t] = outs[h][t]
            return 0

        lax.fori_loop(0, rows_n, step, 0)

    every_ask = remote(asks_v.at[pl.ds(0, rows_n - 1)], asks_v.at[pl.ds(0, rows_n - 1)],
                       asem.at[0], asem.at[1], up, c)
    every_ask.wait_send()
    every_ask.wait_recv()
    to_scalar = pltpu.make_async_copy(asks_v, asks_s, asem.at[2])
    to_scalar.start()
    to_scalar.wait()
    serve(0)
    serve(1)
    serve(2)
    x3.wait_recv()
    x2a.start()
    x1.wait_recv()
    x2b.start()
    place(1, xb1).start()
    place(3, xb3).start()
    serve(3)
    serve(4)
    x2a.wait_recv()
    x2b.wait_recv()
    place(2, xb2).start()
    for j, src in ((0, basis_t), (1, xb1), (3, xb3), (2, xb2)):
        place(j, src).wait()

    to_up = remote(win.at[pl.ds(group, HB)], win.at[pl.ds(0, HB)], hsem.at[0], hsem.at[1], up, c)
    to_down = remote(win.at[pl.ds(HB, HB)], win.at[pl.ds(HB + group, HB)], hsem.at[2], hsem.at[3], down, c)
    to_up.start()
    to_down.start()

    span = group + 2 * HB

    def multiply(first, second, right):
        x = jnp.concatenate([first, second], axis=1)
        a = jnp.concatenate([right[0], right[1]], axis=1)
        return lax.dot_general(x, a, (((1,), (1,)), ((), ())), preferred_element_type=F32)

    def near(k, _):
        n = k // 4

        @pl.when(lax.rem(k, 4) == 0)
        def _():
            band_load(n).wait()

        for t in range(4):
            i = k * 4 + t
            v0 = jnp.clip(slot[0, i], 0, span - 1)
            v1 = jnp.clip(slot[1, i], 0, span - 1)
            pband[i] = multiply(win[v0], win[v1], band_blk[lax.rem(n, 2), lax.rem(k, 4) * 4 + t])

        @pl.when((lax.rem(k, 4) == 3) & (n < group // 16 - 2))
        def _():
            band_load(n + 2).start()

        return 0

    serve(5)
    to_up.wait()
    to_down.wait()
    x1.wait_send()
    x3.wait_send()
    x2a.wait_send()
    x2b.wait_send()
    serve(6)
    lax.fori_loop(0, group // 4, near, 0)
    serve(7)
    far_load.wait()

    def fetched(h):
        count = (rows_n - 1) * per
        remote(fbufs[h].at[pl.ds(0, count)], fbufs[h].at[pl.ds(0, count)],
               osend.at[0, 0], frecv.at[h], up, c).wait_recv()

    limit = rows_n * per - 1

    def arrival(value):
        u = jnp.clip(value - span, 0, limit)
        place_of = lax.rem(lax.div(u, SLOTS) + (cols_n - c), cols_n)
        return lax.div(u, per) * per + place_of * SLOTS + lax.rem(u, SLOTS)

    def whole(h, i):
        first, width = CHUNKS[h]
        far = multiply(fbufs[h][arrival(slot[2, i])], fbufs[h][arrival(slot[3, i])], far_blk[i])
        return pband[i, first:first + width, :] + far

    def diagonal(width):
        return (lax.broadcasted_iota(jnp.int32, (width, size), 0)
                == lax.broadcasted_iota(jnp.int32, (width, size), 1))

    def plain(h, m, t):
        width = CHUNKS[h][1]
        row = rs[h, m, t // PART, pl.ds(lax.rem(t, PART), 1), :]
        scale = jnp.sum(jnp.where(diagonal(width), row, 0.0), axis=1, keepdims=True)
        return rqs[h][m, t].astype(jnp.int32).astype(F32) * scale

    class Message:
        def __init__(self, h, m, d, low, to, relay=None):
            self.h, self.m, self.relay, self.to = h, m, relay, to
            self.first = col_at(d) * own + (0 if low else half)

        def copies(self, part):
            h, m = self.h, self.m
            span_t = pl.ds(part * PART, PART)
            return (remote(sqs[h].at[m, span_t], rqs[h].at[m, span_t], qsend.at[h, m, part],
                           qrecv.at[h, m, part], r, col_at(self.to)),
                    remote(ss.at[h, m, part], rs.at[h, m, part], ssend.at[h, m, part],
                           srecv.at[h, m, part], r, col_at(self.to)))

        def tile(self, t):
            h, m = self.h, self.m
            width = CHUNKS[h][1]
            total = whole(h, self.first + t)
            if self.relay is not None:
                total = total + plain(h, self.relay, t)
            top = jnp.maximum(jnp.max(jnp.abs(total), axis=1, keepdims=True), 1e-30)
            sqs[h][m, t] = jnp.round(total * (FULL / top)).astype(jnp.int32).astype(jnp.int16)
            ss[h, m, t // PART, pl.ds(lax.rem(t, PART), 1), :] = jnp.sum(
                jnp.where(diagonal(width), top * (1.0 / FULL), 0.0), axis=0, keepdims=True)

        def send(self, part):
            for cp in self.copies(part):
                cp.start()

        def arrived(self, part):
            for cp in self.copies(part):
                cp.wait_recv()

        def sent(self):
            for part in range(parts):
                for cp in self.copies(part):
                    cp.wait_send()

    half = own // 2
    parts = half // PART
    mine = c * own

    def messages(h):
        return (Message(h, 0, 2, True, 1), Message(h, 1, 2, False, 3), Message(h, 2, 1, False, 1),
                Message(h, 3, 3, True, 3), Message(h, 4, 1, True, 1, relay=0),
                Message(h, 5, 3, False, 3, relay=1))

    every = [messages(h) for h in range(len(CHUNKS))]

    def keep(h, t):
        first, width = CHUNKS[h]
        pown[t, first:first + width, :] = whole(h, mine + t)

    def add_own(h, pairs):
        first, width = CHUNKS[h]

        def step(t, _):
            for m, high in pairs:
                at = half + t if high else t
                pown[at, first:first + width, :] = pown[at, first:first + width, :] + plain(h, m, t)
            return 0
        lax.fori_loop(0, half, step, 0, unroll=2)

    def run(h, m):
        msg = every[h][m]
        for part in range(parts):
            if msg.relay is not None:
                every[h][msg.relay].arrived(part)

            def step(t, _):
                msg.tile(part * PART + t)
                return 0
            lax.fori_loop(0, PART, step, 0, unroll=4)
            msg.send(part)

    def run_keep(h, low, high):
        def step(t, _):
            keep(h, t)
            return 0
        lax.fori_loop(low, high, step, 0, unroll=4)

    def arrived(h, ms):
        for m in ms:
            for part in range(parts):
                every[h][m].arrived(part)

    def drain(n):
        def step(k, _):
            out_copy(k, n).wait_send()
            return 0
        lax.fori_loop(1, rows_n, step, 0)

    both_halves = ((2, True), (3, False), (4, False), (5, True))
    fetched(0)
    for m in range(4):
        run(0, m)
    run_keep(0, 0, own)
    run(0, 4)
    run(0, 5)
    drain(len(BATCHES) - 2)
    fetched(1)
    for m in range(4):
        run(1, m)
    run_keep(1, 0, own)
    arrived(0, range(2, 6))
    add_own(0, both_halves)
    run(1, 4)
    run(1, 5)
    drain(len(BATCHES) - 1)
    fetched(2)
    for m in range(4):
        run(2, m)
    run_keep(2, 0, PART)
    run(2, 4)
    run(2, 5)
    run_keep(2, PART, own)
    arrived(1, range(2, 6))
    add_own(1, both_halves)
    arrived(2, (2, 3))
    add_own(2, ((2, True), (3, False)))

    last = len(CHUNKS) - 1
    head = CHUNKS[last][0]

    def gram_step(n, total):
        tiles = []
        for t in (2 * n, 2 * n + 1):
            for at, m in ((t, 4), (half + t, 5)):
                p = jnp.concatenate([pown[at, :head, :], pown[at, head:, :] + plain(last, m, t)], axis=0)
                high = p.astype(BF16)
                low = (p - high.astype(F32)).astype(BF16)
                tiles.append(jnp.concatenate([high, low], axis=0))
                part_out[at] = tiles[-1]
        flat = jnp.concatenate(tiles, axis=1)
        return total + lax.dot_general(flat, flat, (((1,), (1,)), ((), ())),
                                       preferred_element_type=F32)

    total = jnp.zeros((2 * size, 2 * size), F32)
    for part in range(parts):
        every[last][4].arrived(part)
        every[last][5].arrived(part)
        total = lax.fori_loop(part * PART // 2, (part + 1) * PART // 2, gram_step, total)
    gram = (total[:size, :size] + total[:size, size:]) + (total[size:, :size] + total[size:, size:])

    slab = size // 8
    gsrc[...] = gram.reshape(8, slab, size)

    core = lax.rem(r, 2)
    base = r - core
    me8 = c * 2 + core

    def eight(e):
        return (base + lax.rem(e, 2), e // 2)

    def pair8(d):
        e = lax.rem(me8 + d, 8)
        return e, eight(e)

    first = []
    for d in range(1, 8):
        e, (row, col) = pair8(d)
        cp = remote(gsrc.at[e], grecv.at[me8], gsend.at[0], gsend.at[1], row, col)
        cp.start()
        first.append(cp)
    grecv[pl.ds(me8, 1)] = gsrc[pl.ds(me8, 1)]
    all7 = remote(grecv.at[pl.ds(0, 7)], grecv.at[pl.ds(0, 7)], gsend.at[0], gsend.at[1], up, c)
    all7.wait_send()
    all7.wait_recv()
    part = grecv[0]
    for e in range(1, 8):
        part = part + grecv[e]
    spot = r // 2
    brecv[pl.ds(spot, 1)] = part[None]
    places = rows_n // 2
    for d in (10, 11, 9, 6, 14, 2, 8, 5, 7, 13, 15, 1, 3, 4, 12):
        oz, oy = d // 4, d % 4
        z, y = r // 8, lax.rem(r // 2, 4)
        row = (lax.rem(z + oz, 4) * 4 + lax.rem(y + oy, 4)) * 2 + core
        remote(brecv.at[spot], brecv.at[spot], gsend.at[2], gsend.at[3], row, c).start()
    all15 = remote(brecv.at[pl.ds(0, places - 1)], brecv.at[pl.ds(0, places - 1)],
                   gsend.at[2], gsend.at[3], up, c)
    all15.wait_send()
    all15.wait_recv()
    part = brecv[0]
    for e in range(1, places):
        part = part + brecv[e]
    crecv[pl.ds(me8, 1)] = part[None]
    for d in range(1, 8):
        e, (row, col) = pair8(d)
        remote(crecv.at[me8], crecv.at[me8], gsend.at[4], gsend.at[5], row, col).start()
    back = remote(crecv.at[pl.ds(0, 7)], crecv.at[pl.ds(0, 7)], gsend.at[4], gsend.at[5], up, c)
    back.wait_send()
    back.wait_recv()
    gram_out[...] = crecv[...].reshape(size, size)
    for chunk in every:
        for msg in chunk:
            msg.sent()


def factorize(gram):
    size = gram.shape[0]
    rows = [gram[8 * i:8 * i + 8, :] for i in range(size // 8)]
    upper = list(rows)
    lane = lax.broadcasted_iota(jnp.int32, (8, size), 1)
    sub = lax.broadcasted_iota(jnp.int32, (8, size), 0)

    def splat(v, k):
        return jnp.broadcast_to(v[:, k:k + 1], (8, size))

    for k in range(0, size, PIVOT):
        vi, s = k // 8, k % 8
        piece = rows[vi]
        r = [jnp.broadcast_to(piece[s + q:s + q + 1, :], (8, size)) for q in range(PIVOT)]
        a = [[splat(r[p], k + q) for q in range(p, PIVOT)] for p in range(PIVOT)]
        block = (lane >= k) & (lane < k + PIVOT)
        rt = [jnp.where(block, jnp.where(lane == k + q, 1.0, 0.0), r[q]) for q in range(PIVOT)]
        low = [[None] * PIVOT for _ in range(PIVOT)]
        inv, scaled, factor = [], [], []
        below = [i for i in range(vi, size // 8) if i > vi or s + PIVOT < 8]
        column = {i: [splat(rows[i], k + q) for q in range(PIVOT)] for i in below}
        new_rows = {i: jnp.where(block, 0.0, rows[i]) for i in below}
        for p in range(PIVOT):
            d = a[p][0]
            for m in range(p):
                d = d - low[p][m] * low[p][m]
            y = lax.rsqrt(d)
            inv.append(y * (1.5 - (0.5 * d * y) * y))
            t, f = rt[p], r[p]
            for m in range(p):
                t = t - low[p][m] * scaled[m]
                f = f - low[p][m] * factor[m]
            scaled.append(t * inv[p])
            factor.append(f * inv[p])
            for i in below:
                t = column[i][p]
                for m in range(p):
                    t = t - low[p][m] * column[i][m]
                column[i][p] = t * inv[p]
                new_rows[i] = new_rows[i] - column[i][p] * scaled[p]
            for n in range(p + 1, PIVOT):
                t = a[p][n - p]
                for m in range(p):
                    t = t - low[n][m] * low[p][m]
                low[n][p] = t * inv[p]
        for i in range(vi, size // 8):
            new = new_rows.get(i, rows[i])
            if i == vi and i in new_rows:
                new = jnp.where(sub >= s + PIVOT, new, rows[i])
            if i == vi:
                up = upper[i] if s else jnp.zeros((8, size), F32)
                for p in range(PIVOT):
                    new = jnp.where((sub == s + p) & (lane <= k + p), scaled[p], new)
                    new = jnp.where((sub == s + p) & (lane > k + p), 0.0, new)
                    up = jnp.where((sub == s + p) & (lane >= k + p), factor[p], up)
                upper[i] = up
            rows[i] = new
    return jnp.concatenate(upper, axis=0), jnp.concatenate(rows, axis=0)


def orthonormalize(scale, gram, product, result, factor, weights):
    rank = gram.shape[0]

    @pl.when(pl.program_id(0) == 0)
    def _():
        upper, inverse = factorize(gram[...] * scale)
        factor[...] = upper
        turned = inverse.T
        high = turned.astype(BF16)
        low = (turned - high.astype(F32)).astype(BF16)
        both = jnp.concatenate([high, low], axis=1)
        weights[...] = jnp.concatenate([both, both], axis=0)

    for t in range(product.shape[0]):
        both = lax.dot_general(product[t], weights[...], (((0,), (0,)), ((), ())),
                               preferred_element_type=F32)
        result[t] = both[:, :rank] + both[:, rank:]


def per_device(rows_n, cols_n, blocks, block_slot, fetch_rows, basis):
    own, size, rank = basis.shape
    group = own * cols_n
    half = own // 2
    parts = half // PART
    per = cols_n * SLOTS
    span = group + 2 * HB
    vmem = pl.BlockSpec(memory_space=pltpu.VMEM)
    tile = (size, rank)
    dma = pltpu.SemaphoreType.DMA
    product, gram = pl.pallas_call(
        functools.partial(kernel, rows_n, cols_n),
        out_shape=(jax.ShapeDtypeStruct((own, 2 * rank, size), BF16),
                   jax.ShapeDtypeStruct((rank, rank), F32)),
        in_specs=[pl.BlockSpec(memory_space=pltpu.SMEM), vmem, vmem, pl.BlockSpec(memory_space=pl.ANY)],
        out_specs=(vmem, vmem),
        scratch_shapes=[
            pltpu.VMEM((rows_n, SLOTS, rows_n * cols_n), jnp.int32),
            pltpu.SMEM((rows_n, SLOTS, rows_n * cols_n), jnp.int32),
            pltpu.VMEM((own,) + tile, BF16),
            pltpu.VMEM((own,) + tile, BF16),
            pltpu.VMEM((own,) + tile, BF16),
            pltpu.VMEM((own,) + tile, BF16),
            pltpu.VMEM((span,) + tile, BF16),
            [pltpu.VMEM((rows_n * per, w, size), BF16) for _, w in CHUNKS],
            [pltpu.VMEM((rows_n * per, w, size), BF16) for _, w in CHUNKS],
            pltpu.VMEM((2, 16, BAND, size, size), BF16),
            pltpu.VMEM((group, 2, size, size), BF16),
            pltpu.VMEM((group,) + tile, F32),
            pltpu.VMEM((own,) + tile, F32),
            [pltpu.VMEM((6, half, w, size), jnp.int16) for _, w in CHUNKS],
            pltpu.VMEM((len(CHUNKS), 6, parts, PART, size), F32),
            [pltpu.VMEM((6, half, w, size), jnp.int16) for _, w in CHUNKS],
            pltpu.VMEM((len(CHUNKS), 6, parts, PART, size), F32),
            pltpu.VMEM((8, rank // 8, rank), F32),
            pltpu.VMEM((8, rank // 8, rank), F32),
            pltpu.VMEM((rows_n // 2, rank // 8, rank), F32),
            pltpu.VMEM((8, rank // 8, rank), F32),
            dma((3,)),
            dma((4,)),
            dma((4,)),
            dma((4,)),
            dma((3,)),
            dma((2, rows_n)),
            dma((len(CHUNKS),)),
            dma((len(CHUNKS), 6, parts)),
            dma((len(CHUNKS), 6, parts)),
            dma((len(CHUNKS), 6, parts)),
            dma((len(CHUNKS), 6, parts)),
            dma((6,)),
            dma((4,)),
        ],
        compiler_params=pltpu.CompilerParams(
            collective_id=0, has_side_effects=True, vmem_limit_bytes=62 * 2**20),
        name="product_and_gram",
    )(block_slot.T, fetch_rows[0].T, basis, blocks)
    total_rows = rows_n * group * size
    steps = 4
    at_once = own // steps
    return tuple(pl.pallas_call(
        functools.partial(orthonormalize, 1.0 / total_rows),
        out_shape=(jax.ShapeDtypeStruct((own,) + tile, F32),
                   jax.ShapeDtypeStruct((rank, rank), F32)),
        grid=(steps,),
        in_specs=[pl.BlockSpec((rank, rank), lambda n: (0, 0)),
                  pl.BlockSpec((at_once, 2 * rank, size), lambda n: (n, 0, 0))],
        out_specs=(pl.BlockSpec((at_once,) + tile, lambda n: (n, 0, 0)),
                   pl.BlockSpec((rank, rank), lambda n: (0, 0))),
        scratch_shapes=[pltpu.VMEM((2 * rank, 2 * rank), BF16)],
        name="orthonormalize",
    )(gram, product))


def solution(mesh):
    in_specs = (
        P("rows", "col", None, None),
        P("rows", "col"),
        P(("rows", "col"), None, None),
        P(("rows", "col"), None, None),
    )
    out_specs = (P(("rows", "col"), None, None), P())
    step = functools.partial(per_device, mesh.shape["rows"], mesh.shape["col"])
    return jax.shard_map(
        step, mesh=mesh, in_specs=in_specs, out_specs=out_specs, check_vma=False
    )
```

```python
import functools

import jax
import jax.numpy as jnp
from jax import lax
from jax.experimental import pallas as pl
from jax.experimental.pallas import tpu as pltpu
from jax.sharding import PartitionSpec as P

HB = 8
BAND = 2
SLOTS = 2
FULL = 32767.0
PIVOT = 8
PART = 8
CHUNKS = ((0, 64), (64, 32), (96, 32))
N_CHUNKS = len(CHUNKS)
BATCHES = (tuple((h, 0, 1) for h in range(N_CHUNKS)) + ((0, 1, 1), (0, 3, 1), (0, 2, 1))
           + tuple((h, j, 1) for h in range(1, N_CHUNKS) for j in (1, 3, 2)))
F32 = jnp.float32
BF16 = jnp.bfloat16


def kernel(rows_n, cols_n, slot, fr, basis, blocks, part_out, gram_out, *scratch):
    (asks_v, asks_s, where_s, basis_t, xb1, xb2, xb3, win, outs, fbufs, band_blk, far_blk, pband, pown,
     sqs, ss, rqs, rs, gsrc, grecv, brecv, crecv,
     asem, hsem, xsend, xrecv, bsem, osend, frecv, qsend, qrecv, ssend, srecv, gsend, wsem) = scratch
    own = basis.shape[0]
    group = own * cols_n
    r = lax.axis_index("rows")
    c = lax.axis_index("col")
    MESH = pl.DeviceIdType.MESH

    def peer(k):
        e = k // 8
        first = 1 - (e + 3) // 4
        turn, oc = lax.rem(k, 4), lax.rem(k // 4, 2)
        cos = (1 - turn) * (1 - lax.rem(turn, 2))
        sin = (2 - turn) * lax.rem(turn, 2)
        y0, z0 = 1 + (3 - e) // 2, (4 - e) // 2
        turned_y, turned_z = cos * y0 - sin * z0, sin * y0 + cos * z0
        flat_y, flat_z = 2 * lax.rem(k // 2, 2), 2 * lax.rem(k // 4, 2)
        oy = first * flat_y + (1 - first) * turned_y
        oz = first * flat_z + (1 - first) * turned_z
        oc = first * lax.rem(k, 2) + (1 - first) * oc
        z, y, core = r // 8, lax.rem(r // 2, 4), lax.rem(r, 2)
        return (lax.rem(z + oz + 4, 4) * 4 + lax.rem(y + oy + 4, 4)) * 2 + lax.rem(core + oc, 2)

    def col_at(d):
        return lax.rem(c + d, cols_n)

    up = lax.rem(r + 1, rows_n)
    down = lax.rem(r + rows_n - 1, rows_n)

    def remote(src, dst, send, recv, row, col):
        return pltpu.make_async_remote_copy(
            src_ref=src, dst_ref=dst, send_sem=send, recv_sem=recv,
            device_id=(row, col), device_id_type=MESH)

    far_load = pltpu.make_async_copy(blocks.at[:, pl.ds(BAND, 2)], far_blk, bsem.at[2])
    far_load.start()

    def band_load(n):
        return pltpu.make_async_copy(
            blocks.at[pl.ds(n * 16, 16), pl.ds(0, BAND)], band_blk.at[lax.rem(n, 2)],
            bsem.at[lax.rem(n, 2)])

    band_load(0).start()
    band_load(1).start()

    barrier = pltpu.get_barrier_semaphore()

    def greet(k, _):
        pl.semaphore_signal(barrier, inc=1, device_id=(peer(k), c), device_id_type=MESH)
        return 0

    lax.fori_loop(1, rows_n, greet, 0)
    beside = r + 1 - 2 * lax.rem(r, 2)
    for d in range(1, cols_n):
        for row in (r, beside):
            pl.semaphore_signal(barrier, inc=1, device_id=(row, col_at(d)), device_id_type=MESH)

    def turn(i, _):
        basis_t[i] = basis[i].T
        return 0

    lax.fori_loop(0, own, turn, 0, unroll=2)
    pl.semaphore_wait(barrier, rows_n - 1 + 2 * (cols_n - 1))

    def ask(k, _):
        p = peer(k)
        remote(fr, asks_v.at[r], asem.at[0], asem.at[1], p, c).start()
        return 0

    lax.fori_loop(1, rows_n, ask, 0)
    asks_v[pl.ds(r, 1)] = fr[...].reshape((1,) + fr.shape)

    x1 = remote(basis_t, xb3, xsend.at[0], xrecv.at[2], r, col_at(1))
    x3 = remote(basis_t, xb1, xsend.at[2], xrecv.at[0], r, col_at(3))
    low, high = pl.ds(0, own // 2), pl.ds(own // 2, own // 2)
    x2a = remote(xb1.at[low], xb2.at[low], xsend.at[1], xrecv.at[1], r, col_at(3))
    x2b = remote(xb3.at[high], xb2.at[high], xsend.at[3], xrecv.at[3], r, col_at(1))
    x1.start()
    x3.start()

    def place(j, src):
        return pltpu.make_async_copy(
            src, win.at[pl.ds(HB + col_at(j) * own, own)], wsem.at[j])

    place(0, basis_t).start()

    size = basis.shape[2]
    per = cols_n * SLOTS

    def out_copy(k, n):
        h, j, count = BATCHES[n]
        at = j * SLOTS
        return remote(outs[h].at[pl.ds(k * per + at, count * SLOTS)],
                      fbufs[h].at[pl.ds(r * per + at, count * SLOTS)],
                      osend.at[n % 2, k], frecv.at[h], peer(k), c)

    def serve(n):
        h, j0, count = BATCHES[n]
        first, width = CHUNKS[h]

        def step(k, _):
            p = peer(k)
            if n > 1:
                @pl.when(k > 0)
                def _():
                    out_copy(k, n - 2).wait_send()
            for j in range(j0, j0 + count):
                src = (basis_t, xb1, xb2, xb3)[j]
                at = r * cols_n + col_at(j)
                for q in range(SLOTS):
                    row = jnp.clip(asks_s[p, q, at], 0, own - 1)
                    outs[h][k * per + j * SLOTS + q] = src[row, first:first + width, :]

            @pl.when(k > 0)
            def _():
                out_copy(k, n).start()

            @pl.when(k == 0)
            def _():
                for t in range(j0 * SLOTS, (j0 + count) * SLOTS):
                    fbufs[h][r * per + t] = outs[h][t]
            return 0

        lax.fori_loop(0, rows_n, step, 0)

    every_ask = remote(asks_v.at[pl.ds(0, rows_n - 1)], asks_v.at[pl.ds(0, rows_n - 1)],
                       asem.at[0], asem.at[1], up, c)
    every_ask.wait_send()
    every_ask.wait_recv()
    to_scalar = pltpu.make_async_copy(asks_v, asks_s, asem.at[2])
    to_scalar.start()
    to_scalar.wait()
    for n in range(N_CHUNKS):
        serve(n)
    x3.wait_recv()
    x2a.start()
    x1.wait_recv()
    x2b.start()
    place(1, xb1).start()
    place(3, xb3).start()
    serve(N_CHUNKS)
    serve(N_CHUNKS + 1)
    x2a.wait_recv()
    x2b.wait_recv()
    place(2, xb2).start()
    for j, src in ((0, basis_t), (1, xb1), (3, xb3), (2, xb2)):
        place(j, src).wait()

    to_up = remote(win.at[pl.ds(group, HB)], win.at[pl.ds(0, HB)], hsem.at[0], hsem.at[1], up, c)
    to_down = remote(win.at[pl.ds(HB, HB)], win.at[pl.ds(HB + group, HB)], hsem.at[2], hsem.at[3], down, c)
    to_up.start()
    to_down.start()

    span = group + 2 * HB

    def multiply(first, second, right):
        x = jnp.concatenate([first, second], axis=1)
        a = jnp.concatenate([right[0], right[1]], axis=1)
        return lax.dot_general(x, a, (((1,), (1,)), ((), ())), preferred_element_type=F32)

    limit = rows_n * per - 1

    def arrival(value):
        u = jnp.clip(value - span, 0, limit)
        place_of = lax.rem(lax.div(u, SLOTS) + (cols_n - c), cols_n)
        return lax.div(u, per) * per + place_of * SLOTS + lax.rem(u, SLOTS)

    def near(k, _):
        n = k // 4

        @pl.when(lax.rem(k, 4) == 0)
        def _():
            band_load(n).wait()

        for t in range(4):
            i = k * 4 + t
            v0 = jnp.clip(slot[0, i], 0, span - 1)
            v1 = jnp.clip(slot[1, i], 0, span - 1)
            for q in range(2):
                where_s[q, i] = arrival(slot[2 + q, i])
            pband[i] = multiply(win[v0], win[v1], band_blk[lax.rem(n, 2), lax.rem(k, 4) * 4 + t])

        @pl.when((lax.rem(k, 4) == 3) & (n < group // 16 - 2))
        def _():
            band_load(n + 2).start()

        return 0

    serve(N_CHUNKS + 2)
    to_up.wait()
    to_down.wait()
    x1.wait_send()
    x3.wait_send()
    x2a.wait_send()
    x2b.wait_send()
    serve(N_CHUNKS + 3)
    lax.fori_loop(0, group // 4, near, 0)
    serve(N_CHUNKS + 4)
    far_load.wait()

    def fetched(h):
        count = (rows_n - 1) * per
        remote(fbufs[h].at[pl.ds(0, count)], fbufs[h].at[pl.ds(0, count)],
               osend.at[0, 0], frecv.at[h], up, c).wait_recv()

    def whole(h, i):
        first, width = CHUNKS[h]
        far = multiply(fbufs[h][where_s[0, i]], fbufs[h][where_s[1, i]], far_blk[i])
        return pband[i, first:first + width, :] + far

    def wholes(h, i0):
        return jnp.stack([whole(h, i0 + t) for t in range(PART)])

    def diagonal(width):
        return (lax.broadcasted_iota(jnp.int32, (PART, width, size), 1)
                == lax.broadcasted_iota(jnp.int32, (PART, width, size), 2))

    def plain(h, m, part):
        width = CHUNKS[h][1]
        row = rs[h, m, part].reshape(PART, 1, size)
        scale = jnp.sum(jnp.where(diagonal(width), row, 0.0), axis=2, keepdims=True)
        return rqs[h][m, pl.ds(part * PART, PART)].astype(jnp.int32).astype(F32) * scale

    class Message:
        def __init__(self, h, m, d, low, to, relay=None):
            self.h, self.m, self.relay, self.to = h, m, relay, to
            self.first = col_at(d) * own + (0 if low else half)

        def copies(self, part):
            h, m = self.h, self.m
            span_t = pl.ds(part * PART, PART)
            return (remote(sqs[h].at[m, span_t], rqs[h].at[m, span_t], qsend.at[h, m, part],
                           qrecv.at[h, m, part], r, col_at(self.to)),
                    remote(ss.at[h, m, part], rs.at[h, m, part], ssend.at[h, m, part],
                           srecv.at[h, m, part], r, col_at(self.to)))

        def code(self, part):
            h, m = self.h, self.m
            width = CHUNKS[h][1]
            total = wholes(h, self.first + part * PART)
            if self.relay is not None:
                total = total + plain(h, self.relay, part)
            top = jnp.maximum(jnp.max(jnp.abs(total), axis=2, keepdims=True), 1e-30)
            sqs[h][m, pl.ds(part * PART, PART)] = (
                jnp.round(total * (FULL / top)).astype(jnp.int32).astype(jnp.int16))
            ss[h, m, part] = jnp.sum(jnp.where(diagonal(width), top * (1.0 / FULL), 0.0), axis=1)

        def send(self, part):
            for cp in self.copies(part):
                cp.start()

        def arrived(self, part):
            for cp in self.copies(part):
                cp.wait_recv()

        def sent(self):
            for part in range(parts):
                for cp in self.copies(part):
                    cp.wait_send()

    half = own // 2
    parts = half // PART
    mine = c * own

    def messages(h):
        return (Message(h, 0, 2, True, 1), Message(h, 1, 2, False, 3), Message(h, 2, 1, False, 1),
                Message(h, 3, 3, True, 3), Message(h, 4, 1, True, 1, relay=0),
                Message(h, 5, 3, False, 3, relay=1))

    every = [messages(h) for h in range(N_CHUNKS)]

    def add_own(h, pairs):
        first, width = CHUNKS[h]

        def step(part, _):
            for m, high in pairs:
                at = pl.ds((half if high else 0) + part * PART, PART)
                pown[at, first:first + width, :] = pown[at, first:first + width, :] + plain(h, m, part)
            return 0
        lax.fori_loop(0, parts, step, 0)

    def run(h, m):
        msg = every[h][m]

        def step(part, _):
            if msg.relay is not None:
                every[h][msg.relay].arrived(part)
            msg.code(part)
            msg.send(part)
            return 0
        lax.fori_loop(0, parts, step, 0)

    def run_keep(h, low, high):
        first, width = CHUNKS[h]

        def step(part, _):
            pown[pl.ds(part * PART, PART), first:first + width, :] = wholes(h, mine + part * PART)
            return 0
        lax.fori_loop(low // PART, high // PART, step, 0)

    def arrived(h, ms):
        for m in ms:
            for part in range(parts):
                every[h][m].arrived(part)

    def drain(n):
        def step(k, _):
            out_copy(k, n).wait_send()
            return 0
        lax.fori_loop(1, rows_n, step, 0)

    both_halves = ((2, True), (3, False), (4, False), (5, True))
    last = N_CHUNKS - 1
    fetched(0)
    run(0, 0)
    run(0, 1)
    serve(N_CHUNKS + 5)
    run(0, 2)
    run(0, 3)
    serve(N_CHUNKS + 6)
    run_keep(0, 0, own)
    serve(N_CHUNKS + 7)
    run(0, 4)
    run(0, 5)
    for n in range(N_CHUNKS + 8, len(BATCHES)):
        serve(n)
    for h in range(1, last):
        fetched(h)
        for m in range(4):
            run(h, m)
        run_keep(h, 0, own)
        arrived(h - 1, range(2, 6))
        add_own(h - 1, both_halves)
        run(h, 4)
        run(h, 5)
    drain(len(BATCHES) - 2)
    drain(len(BATCHES) - 1)
    fetched(last)
    for m in range(4):
        run(last, m)
    run_keep(last, 0, PART)
    run(last, 4)
    run(last, 5)
    run_keep(last, PART, own)
    arrived(last - 1, range(2, 6))
    add_own(last - 1, both_halves)
    arrived(last, (2, 3))
    add_own(last, ((2, True), (3, False)))

    head = CHUNKS[last][0]

    def gram_step(part, total):
        every[last][4].arrived(part)
        every[last][5].arrived(part)
        for at, m in ((0, 4), (half, 5)):
            at = pl.ds(at + part * PART, PART)
            pown[at, head:, :] = pown[at, head:, :] + plain(last, m, part)
        for t0 in range(0, PART, 2):
            tiles = []
            for at in (part * PART + t0, part * PART + t0 + 1,
                       half + part * PART + t0, half + part * PART + t0 + 1):
                p = pown[at]
                high = p.astype(BF16)
                low = (p - high.astype(F32)).astype(BF16)
                tiles.append(jnp.concatenate([high, low], axis=0))
                part_out[at] = tiles[-1]
            flat = jnp.concatenate(tiles, axis=1)
            total = total + lax.dot_general(flat, flat, (((1,), (1,)), ((), ())),
                                            preferred_element_type=F32)
        return total

    total = lax.fori_loop(0, parts, gram_step, jnp.zeros((2 * size, 2 * size), F32))
    gram = (total[:size, :size] + total[:size, size:]) + (total[size:, :size] + total[size:, size:])

    slab = size // 8
    gsrc[...] = gram.reshape(8, slab, size)

    core = lax.rem(r, 2)
    base = r - core
    me8 = c * 2 + core

    def eight(e):
        return (base + lax.rem(e, 2), e // 2)

    def pair8(d):
        e = lax.rem(me8 + d, 8)
        return e, eight(e)

    first = []
    for d in range(1, 8):
        e, (row, col) = pair8(d)
        cp = remote(gsrc.at[e], grecv.at[me8], gsend.at[0], gsend.at[1], row, col)
        cp.start()
        first.append(cp)
    grecv[pl.ds(me8, 1)] = gsrc[pl.ds(me8, 1)]
    all7 = remote(grecv.at[pl.ds(0, 7)], grecv.at[pl.ds(0, 7)], gsend.at[0], gsend.at[1], up, c)
    all7.wait_send()
    all7.wait_recv()
    part = grecv[0]
    for e in range(1, 8):
        part = part + grecv[e]
    spot = r // 2
    brecv[pl.ds(spot, 1)] = part[None]
    places = rows_n // 2
    for d in (10, 11, 9, 6, 14, 2, 8, 5, 7, 13, 15, 1, 3, 4, 12):
        oz, oy = d // 4, d % 4
        z, y = r // 8, lax.rem(r // 2, 4)
        row = (lax.rem(z + oz, 4) * 4 + lax.rem(y + oy, 4)) * 2 + core
        remote(brecv.at[spot], brecv.at[spot], gsend.at[2], gsend.at[3], row, c).start()
    all15 = remote(brecv.at[pl.ds(0, places - 1)], brecv.at[pl.ds(0, places - 1)],
                   gsend.at[2], gsend.at[3], up, c)
    all15.wait_send()
    all15.wait_recv()
    part = brecv[0]
    for e in range(1, places):
        part = part + brecv[e]
    crecv[pl.ds(me8, 1)] = part[None]
    for d in range(1, 8):
        e, (row, col) = pair8(d)
        remote(crecv.at[me8], crecv.at[me8], gsend.at[4], gsend.at[5], row, col).start()
    back = remote(crecv.at[pl.ds(0, 7)], crecv.at[pl.ds(0, 7)], gsend.at[4], gsend.at[5], up, c)
    back.wait_send()
    back.wait_recv()
    gram_out[...] = crecv[...].reshape(size, size)
    for chunk in every:
        for msg in chunk:
            msg.sent()


def factorize(gram):
    size = gram.shape[0]
    rows = [gram[8 * i:8 * i + 8, :] for i in range(size // 8)]
    upper = list(rows)
    lane = lax.broadcasted_iota(jnp.int32, (8, size), 1)
    sub = lax.broadcasted_iota(jnp.int32, (8, size), 0)

    def splat(v, k):
        return jnp.broadcast_to(v[:, k:k + 1], (8, size))

    for k in range(0, size, PIVOT):
        vi, s = k // 8, k % 8
        piece = rows[vi]
        r = [jnp.broadcast_to(piece[s + q:s + q + 1, :], (8, size)) for q in range(PIVOT)]
        a = [[splat(r[p], k + q) for q in range(p, PIVOT)] for p in range(PIVOT)]
        block = (lane >= k) & (lane < k + PIVOT)
        rt = [jnp.where(block, jnp.where(lane == k + q, 1.0, 0.0), r[q]) for q in range(PIVOT)]
        low = [[None] * PIVOT for _ in range(PIVOT)]
        inv, scaled, factor = [], [], []
        below = [i for i in range(vi, size // 8) if i > vi or s + PIVOT < 8]
        column = {i: [splat(rows[i], k + q) for q in range(PIVOT)] for i in below}
        new_rows = {i: jnp.where(block, 0.0, rows[i]) for i in below}
        for p in range(PIVOT):
            d = a[p][0]
            for m in range(p):
                d = d - low[p][m] * low[p][m]
            y = lax.rsqrt(d)
            inv.append(y * (1.5 - (0.5 * d * y) * y))
            t, f = rt[p], r[p]
            for m in range(p):
                t = t - low[p][m] * scaled[m]
                f = f - low[p][m] * factor[m]
            scaled.append(t * inv[p])
            factor.append(f * inv[p])
            for i in below:
                t = column[i][p]
                for m in range(p):
                    t = t - low[p][m] * column[i][m]
                column[i][p] = t * inv[p]
                new_rows[i] = new_rows[i] - column[i][p] * scaled[p]
            for n in range(p + 1, PIVOT):
                t = a[p][n - p]
                for m in range(p):
                    t = t - low[n][m] * low[p][m]
                low[n][p] = t * inv[p]
        for i in range(vi, size // 8):
            new = new_rows.get(i, rows[i])
            if i == vi and i in new_rows:
                new = jnp.where(sub >= s + PIVOT, new, rows[i])
            if i == vi:
                up = upper[i] if s else jnp.zeros((8, size), F32)
                for p in range(PIVOT):
                    new = jnp.where((sub == s + p) & (lane <= k + p), scaled[p], new)
                    new = jnp.where((sub == s + p) & (lane > k + p), 0.0, new)
                    up = jnp.where((sub == s + p) & (lane >= k + p), factor[p], up)
                upper[i] = up
            rows[i] = new
    return jnp.concatenate(upper, axis=0), jnp.concatenate(rows, axis=0)


def orthonormalize(scale, gram, product, result, factor, weights):
    rank = gram.shape[0]

    @pl.when(pl.program_id(0) == 0)
    def _():
        upper, inverse = factorize(gram[...] * scale)
        factor[...] = upper
        turned = inverse.T
        high = turned.astype(BF16)
        low = (turned - high.astype(F32)).astype(BF16)
        both = jnp.concatenate([high, low], axis=1)
        weights[...] = jnp.concatenate([both, both], axis=0)

    for t in range(product.shape[0]):
        both = lax.dot_general(product[t], weights[...], (((0,), (0,)), ((), ())),
                               preferred_element_type=F32)
        result[t] = both[:, :rank] + both[:, rank:]


def per_device(rows_n, cols_n, blocks, block_slot, fetch_rows, basis):
    own, size, rank = basis.shape
    group = own * cols_n
    half = own // 2
    parts = half // PART
    per = cols_n * SLOTS
    span = group + 2 * HB
    vmem = pl.BlockSpec(memory_space=pltpu.VMEM)
    tile = (size, rank)
    dma = pltpu.SemaphoreType.DMA
    product, gram = pl.pallas_call(
        functools.partial(kernel, rows_n, cols_n),
        out_shape=(jax.ShapeDtypeStruct((own, 2 * rank, size), BF16),
                   jax.ShapeDtypeStruct((rank, rank), F32)),
        in_specs=[pl.BlockSpec(memory_space=pltpu.SMEM), vmem, vmem, pl.BlockSpec(memory_space=pl.ANY)],
        out_specs=(vmem, vmem),
        scratch_shapes=[
            pltpu.VMEM((rows_n, SLOTS, rows_n * cols_n), jnp.int32),
            pltpu.SMEM((rows_n, SLOTS, rows_n * cols_n), jnp.int32),
            pltpu.SMEM((2, group), jnp.int32),
            pltpu.VMEM((own,) + tile, BF16),
            pltpu.VMEM((own,) + tile, BF16),
            pltpu.VMEM((own,) + tile, BF16),
            pltpu.VMEM((own,) + tile, BF16),
            pltpu.VMEM((span,) + tile, BF16),
            [pltpu.VMEM((rows_n * per, w, size), BF16) for _, w in CHUNKS],
            [pltpu.VMEM((rows_n * per, w, size), BF16) for _, w in CHUNKS],
            pltpu.VMEM((2, 16, BAND, size, size), BF16),
            pltpu.VMEM((group, 2, size, size), BF16),
            pltpu.VMEM((group,) + tile, F32),
            pltpu.VMEM((own,) + tile, F32),
            [pltpu.VMEM((6, half, w, size), jnp.int16) for _, w in CHUNKS],
            pltpu.VMEM((N_CHUNKS, 6, parts, PART, size), F32),
            [pltpu.VMEM((6, half, w, size), jnp.int16) for _, w in CHUNKS],
            pltpu.VMEM((N_CHUNKS, 6, parts, PART, size), F32),
            pltpu.VMEM((8, rank // 8, rank), F32),
            pltpu.VMEM((8, rank // 8, rank), F32),
            pltpu.VMEM((rows_n // 2, rank // 8, rank), F32),
            pltpu.VMEM((8, rank // 8, rank), F32),
            dma((3,)),
            dma((4,)),
            dma((4,)),
            dma((4,)),
            dma((3,)),
            dma((2, rows_n)),
            dma((N_CHUNKS,)),
            dma((N_CHUNKS, 6, parts)),
            dma((N_CHUNKS, 6, parts)),
            dma((N_CHUNKS, 6, parts)),
            dma((N_CHUNKS, 6, parts)),
            dma((6,)),
            dma((4,)),
        ],
        compiler_params=pltpu.CompilerParams(
            collective_id=0, has_side_effects=True, vmem_limit_bytes=62 * 2**20),
        name="product_and_gram",
    )(block_slot.T, fetch_rows[0].T, basis, blocks)
    total_rows = rows_n * group * size
    steps = 4
    at_once = own // steps
    return tuple(pl.pallas_call(
        functools.partial(orthonormalize, 1.0 / total_rows),
        out_shape=(jax.ShapeDtypeStruct((own,) + tile, F32),
                   jax.ShapeDtypeStruct((rank, rank), F32)),
        grid=(steps,),
        in_specs=[pl.BlockSpec((rank, rank), lambda n: (0, 0)),
                  pl.BlockSpec((at_once, 2 * rank, size), lambda n: (n, 0, 0))],
        out_specs=(pl.BlockSpec((at_once,) + tile, lambda n: (n, 0, 0)),
                   pl.BlockSpec((rank, rank), lambda n: (0, 0))),
        scratch_shapes=[pltpu.VMEM((2 * rank, 2 * rank), BF16)],
        name="orthonormalize",
    )(gram, product))


def solution(mesh):
    in_specs = (
        P("rows", "col", None, None),
        P("rows", "col"),
        P(("rows", "col"), None, None),
        P(("rows", "col"), None, None),
    )
    out_specs = (P(("rows", "col"), None, None), P())
    step = functools.partial(per_device, mesh.shape["rows"], mesh.shape["col"])
    return jax.shard_map(
        step, mesh=mesh, in_specs=in_specs, out_specs=out_specs, check_vma=False
    )
```

```python
import functools

import jax
import jax.numpy as jnp
from jax import lax
from jax.experimental import pallas as pl
from jax.experimental.pallas import tpu as pltpu
from jax.sharding import PartitionSpec as P

HB = 8
BAND = 2
SLOTS = 2
FULL = 32767.0
PIVOT = 8
PART = 16
CHUNKS = ((0, 64), (64, 32), (96, 32))
N_CHUNKS = len(CHUNKS)
BATCHES = (tuple((h, 0, 1) for h in range(N_CHUNKS)) + ((0, 1, 1), (0, 3, 1), (0, 2, 1))
           + tuple((h, j, 1) for h in range(1, N_CHUNKS) for j in (1, 3, 2)))
F32 = jnp.float32
BF16 = jnp.bfloat16


def kernel(rows_n, cols_n, slot, fr, basis, blocks, part_out, gram_out, *scratch):
    (asks_v, asks_s, where_s, basis_t, xb1, xb2, xb3, win, outs, fbufs, band_blk, far_blk, pband, pown,
     sqs, ss, rqs, rs, gsrc, grecv, brecv, crecv,
     asem, hsem, xsend, xrecv, bsem, osend, frecv, qsend, qrecv, ssend, srecv, gsend, wsem) = scratch
    own = basis.shape[0]
    group = own * cols_n
    r = lax.axis_index("rows")
    c = lax.axis_index("col")
    MESH = pl.DeviceIdType.MESH

    def peer(k):
        e = k // 8
        first = 1 - (e + 3) // 4
        turn, oc = lax.rem(k, 4), lax.rem(k // 4, 2)
        cos = (1 - turn) * (1 - lax.rem(turn, 2))
        sin = (2 - turn) * lax.rem(turn, 2)
        y0, z0 = 1 + (3 - e) // 2, (4 - e) // 2
        turned_y, turned_z = cos * y0 - sin * z0, sin * y0 + cos * z0
        flat_y, flat_z = 2 * lax.rem(k // 2, 2), 2 * lax.rem(k // 4, 2)
        oy = first * flat_y + (1 - first) * turned_y
        oz = first * flat_z + (1 - first) * turned_z
        oc = first * lax.rem(k, 2) + (1 - first) * oc
        z, y, core = r // 8, lax.rem(r // 2, 4), lax.rem(r, 2)
        return (lax.rem(z + oz + 4, 4) * 4 + lax.rem(y + oy + 4, 4)) * 2 + lax.rem(core + oc, 2)

    def col_at(d):
        return lax.rem(c + d, cols_n)

    up = lax.rem(r + 1, rows_n)
    down = lax.rem(r + rows_n - 1, rows_n)

    def remote(src, dst, send, recv, row, col):
        return pltpu.make_async_remote_copy(
            src_ref=src, dst_ref=dst, send_sem=send, recv_sem=recv,
            device_id=(row, col), device_id_type=MESH)

    far_load = pltpu.make_async_copy(blocks.at[:, pl.ds(BAND, 2)], far_blk, bsem.at[2])
    far_load.start()

    def band_load(n):
        return pltpu.make_async_copy(
            blocks.at[pl.ds(n * 16, 16), pl.ds(0, BAND)], band_blk.at[lax.rem(n, 2)],
            bsem.at[lax.rem(n, 2)])

    band_load(0).start()
    band_load(1).start()

    barrier = pltpu.get_barrier_semaphore()

    def greet(k, _):
        pl.semaphore_signal(barrier, inc=1, device_id=(peer(k), c), device_id_type=MESH)
        return 0

    lax.fori_loop(1, rows_n, greet, 0)
    beside = r + 1 - 2 * lax.rem(r, 2)
    for d in range(1, cols_n):
        for row in (r, beside):
            pl.semaphore_signal(barrier, inc=1, device_id=(row, col_at(d)), device_id_type=MESH)

    pl.semaphore_wait(barrier, rows_n - 1 + 2 * (cols_n - 1))

    def ask(k, _):
        p = peer(k)
        remote(fr, asks_v.at[r], asem.at[0], asem.at[1], p, c).start()
        return 0

    lax.fori_loop(1, rows_n, ask, 0)
    asks_v[pl.ds(r, 1)] = fr[...].reshape((1,) + fr.shape)
    def turn(i, _):
        basis_t[i] = basis[i].T
        return 0

    lax.fori_loop(0, own, turn, 0, unroll=2)

    x1 = remote(basis_t, xb3, xsend.at[0], xrecv.at[2], r, col_at(1))
    x3 = remote(basis_t, xb1, xsend.at[2], xrecv.at[0], r, col_at(3))
    low, high = pl.ds(0, own // 2), pl.ds(own // 2, own // 2)
    x2a = remote(xb1.at[low], xb2.at[low], xsend.at[1], xrecv.at[1], r, col_at(3))
    x2b = remote(xb3.at[high], xb2.at[high], xsend.at[3], xrecv.at[3], r, col_at(1))
    x1.start()
    x3.start()

    def place(j, src):
        return pltpu.make_async_copy(
            src, win.at[pl.ds(HB + col_at(j) * own, own)], wsem.at[j])

    place(0, basis_t).start()

    size = basis.shape[2]
    per = cols_n * SLOTS

    def out_copy(k, n):
        h, j, count = BATCHES[n]
        at = j * SLOTS
        return remote(outs[h].at[pl.ds(k * per + at, count * SLOTS)],
                      fbufs[h].at[pl.ds(r * per + at, count * SLOTS)],
                      osend.at[n % 2, k], frecv.at[h], peer(k), c)

    def serve(n):
        h, j0, count = BATCHES[n]
        first, width = CHUNKS[h]

        def step(k, _):
            p = peer(k)
            if n > 1:
                @pl.when(k > 0)
                def _():
                    out_copy(k, n - 2).wait_send()
            for j in range(j0, j0 + count):
                src = (basis_t, xb1, xb2, xb3)[j]
                at = r * cols_n + col_at(j)
                for q in range(SLOTS):
                    row = jnp.clip(asks_s[p, q, at], 0, own - 1)
                    outs[h][k * per + j * SLOTS + q] = src[row, first:first + width, :]

            @pl.when(k > 0)
            def _():
                out_copy(k, n).start()

            @pl.when(k == 0)
            def _():
                for t in range(j0 * SLOTS, (j0 + count) * SLOTS):
                    fbufs[h][r * per + t] = outs[h][t]
            return 0

        lax.fori_loop(0, rows_n, step, 0)

    every_ask = remote(asks_v.at[pl.ds(0, rows_n - 1)], asks_v.at[pl.ds(0, rows_n - 1)],
                       asem.at[0], asem.at[1], up, c)
    every_ask.wait_send()
    every_ask.wait_recv()
    to_scalar = pltpu.make_async_copy(asks_v, asks_s, asem.at[2])
    to_scalar.start()
    to_scalar.wait()
    for n in range(N_CHUNKS):
        serve(n)
    x3.wait_recv()
    x2a.start()
    x1.wait_recv()
    x2b.start()
    place(1, xb1).start()
    place(3, xb3).start()
    serve(N_CHUNKS)
    serve(N_CHUNKS + 1)
    x2a.wait_recv()
    x2b.wait_recv()
    place(2, xb2).start()
    for j, src in ((0, basis_t), (1, xb1), (3, xb3), (2, xb2)):
        place(j, src).wait()

    to_up = remote(win.at[pl.ds(group, HB)], win.at[pl.ds(0, HB)], hsem.at[0], hsem.at[1], up, c)
    to_down = remote(win.at[pl.ds(HB, HB)], win.at[pl.ds(HB + group, HB)], hsem.at[2], hsem.at[3], down, c)
    to_up.start()
    to_down.start()

    span = group + 2 * HB

    def multiply(first, second, right):
        x = jnp.concatenate([first, second], axis=1)
        a = jnp.concatenate([right[0], right[1]], axis=1)
        return lax.dot_general(x, a, (((1,), (1,)), ((), ())), preferred_element_type=F32)

    limit = rows_n * per - 1

    def arrival(value):
        u = jnp.clip(value - span, 0, limit)
        place_of = lax.rem(lax.div(u, SLOTS) + (cols_n - c), cols_n)
        return lax.div(u, per) * per + place_of * SLOTS + lax.rem(u, SLOTS)

    def near(k, _):
        n = k // 4

        @pl.when(lax.rem(k, 4) == 0)
        def _():
            band_load(n).wait()

        for t in range(4):
            i = k * 4 + t
            v0 = jnp.clip(slot[0, i], 0, span - 1)
            v1 = jnp.clip(slot[1, i], 0, span - 1)
            for q in range(2):
                where_s[q, i] = arrival(slot[2 + q, i])
            pband[i] = multiply(win[v0], win[v1], band_blk[lax.rem(n, 2), lax.rem(k, 4) * 4 + t])

        @pl.when((lax.rem(k, 4) == 3) & (n < group // 16 - 2))
        def _():
            band_load(n + 2).start()

        return 0

    serve(N_CHUNKS + 2)
    to_up.wait()
    to_down.wait()
    x1.wait_send()
    x3.wait_send()
    x2a.wait_send()
    x2b.wait_send()
    serve(N_CHUNKS + 3)
    lax.fori_loop(0, group // 4, near, 0)
    serve(N_CHUNKS + 4)
    far_load.wait()

    def fetched(h):
        count = (rows_n - 1) * per
        remote(fbufs[h].at[pl.ds(0, count)], fbufs[h].at[pl.ds(0, count)],
               osend.at[0, 0], frecv.at[h], up, c).wait_recv()

    def whole(h, i):
        first, width = CHUNKS[h]
        far = multiply(fbufs[h][where_s[0, i]], fbufs[h][where_s[1, i]], far_blk[i])
        return pband[i, first:first + width, :] + far

    def wholes(h, i0):
        return jnp.stack([whole(h, i0 + t) for t in range(PART)])

    def diagonal(width):
        return (lax.broadcasted_iota(jnp.int32, (PART, width, size), 1)
                == lax.broadcasted_iota(jnp.int32, (PART, width, size), 2))

    def plain(h, m, part):
        width = CHUNKS[h][1]
        row = rs[h, m, part].reshape(PART, 1, size)
        scale = jnp.sum(jnp.where(diagonal(width), row, 0.0), axis=2, keepdims=True)
        return rqs[h][m, pl.ds(part * PART, PART)].astype(jnp.int32).astype(F32) * scale

    class Message:
        def __init__(self, h, m, d, low, to, relay=None):
            self.h, self.m, self.relay, self.to = h, m, relay, to
            self.first = col_at(d) * own + (0 if low else half)

        def copies(self, part):
            h, m = self.h, self.m
            span_t = pl.ds(part * PART, PART)
            return (remote(sqs[h].at[m, span_t], rqs[h].at[m, span_t], qsend.at[h, m, part],
                           qrecv.at[h, m, part], r, col_at(self.to)),
                    remote(ss.at[h, m, part], rs.at[h, m, part], ssend.at[h, m, part],
                           srecv.at[h, m, part], r, col_at(self.to)))

        def code(self, part):
            h, m = self.h, self.m
            width = CHUNKS[h][1]
            total = wholes(h, self.first + part * PART)
            if self.relay is not None:
                total = total + plain(h, self.relay, part)
            top = jnp.maximum(jnp.max(jnp.abs(total), axis=2, keepdims=True), 1e-30)
            sqs[h][m, pl.ds(part * PART, PART)] = (
                jnp.round(total * (FULL / top)).astype(jnp.int32).astype(jnp.int16))
            ss[h, m, part] = jnp.sum(jnp.where(diagonal(width), top * (1.0 / FULL), 0.0), axis=1)

        def send(self, part):
            for cp in self.copies(part):
                cp.start()

        def arrived(self, part):
            for cp in self.copies(part):
                cp.wait_recv()

        def sent(self):
            for part in range(parts):
                for cp in self.copies(part):
                    cp.wait_send()

    half = own // 2
    parts = half // PART
    mine = c * own

    def messages(h):
        return (Message(h, 0, 2, True, 1), Message(h, 1, 2, False, 3), Message(h, 2, 1, False, 1),
                Message(h, 3, 3, True, 3), Message(h, 4, 1, True, 1, relay=0),
                Message(h, 5, 3, False, 3, relay=1))

    every = [messages(h) for h in range(N_CHUNKS)]

    def add_own(h, pairs):
        first, width = CHUNKS[h]

        def step(part, _):
            for m, high in pairs:
                at = pl.ds((half if high else 0) + part * PART, PART)
                pown[at, first:first + width, :] = pown[at, first:first + width, :] + plain(h, m, part)
            return 0
        lax.fori_loop(0, parts, step, 0)

    def run(h, m):
        msg = every[h][m]

        def step(part, _):
            if msg.relay is not None:
                every[h][msg.relay].arrived(part)
            msg.code(part)
            msg.send(part)
            return 0
        lax.fori_loop(0, parts, step, 0)

    def run_keep(h, low, high):
        first, width = CHUNKS[h]

        def step(part, _):
            pown[pl.ds(part * PART, PART), first:first + width, :] = wholes(h, mine + part * PART)
            return 0
        lax.fori_loop(low // PART, high // PART, step, 0)

    def arrived(h, ms):
        for m in ms:
            for part in range(parts):
                every[h][m].arrived(part)

    def drain(n):
        def step(k, _):
            out_copy(k, n).wait_send()
            return 0
        lax.fori_loop(1, rows_n, step, 0)

    both_halves = ((2, True), (3, False), (4, False), (5, True))
    last = N_CHUNKS - 1
    fetched(0)
    run(0, 0)
    run(0, 1)
    serve(N_CHUNKS + 5)
    run(0, 2)
    run(0, 3)
    serve(N_CHUNKS + 6)
    run_keep(0, 0, own)
    serve(N_CHUNKS + 7)
    run(0, 4)
    run(0, 5)
    for n in range(N_CHUNKS + 8, len(BATCHES)):
        serve(n)
    for h in range(1, last):
        fetched(h)
        for m in range(4):
            run(h, m)
        run_keep(h, 0, own)
        arrived(h - 1, range(2, 6))
        add_own(h - 1, both_halves)
        run(h, 4)
        run(h, 5)
    drain(len(BATCHES) - 2)
    drain(len(BATCHES) - 1)
    fetched(last)
    for m in range(4):
        run(last, m)
    run_keep(last, 0, PART)
    run(last, 4)
    run(last, 5)
    run_keep(last, PART, own)
    arrived(last - 1, range(2, 6))
    add_own(last - 1, both_halves)
    arrived(last, (2, 3))
    add_own(last, ((2, True), (3, False)))

    head = CHUNKS[last][0]

    def gram_step(part, total):
        every[last][4].arrived(part)
        every[last][5].arrived(part)
        for at, m in ((0, 4), (half, 5)):
            at = pl.ds(at + part * PART, PART)
            pown[at, head:, :] = pown[at, head:, :] + plain(last, m, part)
        for t0 in range(0, PART, 2):
            tiles = []
            for at in (part * PART + t0, part * PART + t0 + 1,
                       half + part * PART + t0, half + part * PART + t0 + 1):
                p = pown[at]
                high = p.astype(BF16)
                low = (p - high.astype(F32)).astype(BF16)
                tiles.append(jnp.concatenate([high, low], axis=0))
                part_out[at] = tiles[-1]
            flat = jnp.concatenate(tiles, axis=1)
            total = total + lax.dot_general(flat, flat, (((1,), (1,)), ((), ())),
                                            preferred_element_type=F32)
        return total

    total = lax.fori_loop(0, parts, gram_step, jnp.zeros((2 * size, 2 * size), F32))
    gram = (total[:size, :size] + total[:size, size:]) + (total[size:, :size] + total[size:, size:])

    slab = size // 8
    gsrc[...] = gram.reshape(8, slab, size)

    core = lax.rem(r, 2)
    base = r - core
    me8 = c * 2 + core

    def eight(e):
        return (base + lax.rem(e, 2), e // 2)

    def pair8(d):
        e = lax.rem(me8 + d, 8)
        return e, eight(e)

    first = []
    for d in range(1, 8):
        e, (row, col) = pair8(d)
        cp = remote(gsrc.at[e], grecv.at[me8], gsend.at[0], gsend.at[1], row, col)
        cp.start()
        first.append(cp)
    grecv[pl.ds(me8, 1)] = gsrc[pl.ds(me8, 1)]
    all7 = remote(grecv.at[pl.ds(0, 7)], grecv.at[pl.ds(0, 7)], gsend.at[0], gsend.at[1], up, c)
    all7.wait_send()
    all7.wait_recv()
    part = grecv[0]
    for e in range(1, 8):
        part = part + grecv[e]
    spot = r // 2
    brecv[pl.ds(spot, 1)] = part[None]
    places = rows_n // 2
    for d in (10, 11, 9, 6, 14, 2, 8, 5, 7, 13, 15, 1, 3, 4, 12):
        oz, oy = d // 4, d % 4
        z, y = r // 8, lax.rem(r // 2, 4)
        row = (lax.rem(z + oz, 4) * 4 + lax.rem(y + oy, 4)) * 2 + core
        remote(brecv.at[spot], brecv.at[spot], gsend.at[2], gsend.at[3], row, c).start()
    all15 = remote(brecv.at[pl.ds(0, places - 1)], brecv.at[pl.ds(0, places - 1)],
                   gsend.at[2], gsend.at[3], up, c)
    all15.wait_send()
    all15.wait_recv()
    part = brecv[0]
    for e in range(1, places):
        part = part + brecv[e]
    crecv[pl.ds(me8, 1)] = part[None]
    for d in range(1, 8):
        e, (row, col) = pair8(d)
        remote(crecv.at[me8], crecv.at[me8], gsend.at[4], gsend.at[5], row, col).start()
    back = remote(crecv.at[pl.ds(0, 7)], crecv.at[pl.ds(0, 7)], gsend.at[4], gsend.at[5], up, c)
    back.wait_send()
    back.wait_recv()
    gram_out[...] = crecv[...].reshape(size, size)
    for chunk in every:
        for msg in chunk:
            msg.sent()


def factorize(gram):
    size = gram.shape[0]
    rows = [gram[8 * i:8 * i + 8, :] for i in range(size // 8)]
    upper = list(rows)
    lane = lax.broadcasted_iota(jnp.int32, (8, size), 1)
    sub = lax.broadcasted_iota(jnp.int32, (8, size), 0)

    def splat(v, k):
        return jnp.broadcast_to(v[:, k:k + 1], (8, size))

    for k in range(0, size, PIVOT):
        vi, s = k // 8, k % 8
        piece = rows[vi]
        r = [jnp.broadcast_to(piece[s + q:s + q + 1, :], (8, size)) for q in range(PIVOT)]
        a = [[splat(r[p], k + q) for q in range(p, PIVOT)] for p in range(PIVOT)]
        block = (lane >= k) & (lane < k + PIVOT)
        rt = [jnp.where(block, jnp.where(lane == k + q, 1.0, 0.0), r[q]) for q in range(PIVOT)]
        low = [[None] * PIVOT for _ in range(PIVOT)]
        inv, scaled, factor = [], [], []
        below = [i for i in range(vi, size // 8) if i > vi or s + PIVOT < 8]
        column = {i: [splat(rows[i], k + q) for q in range(PIVOT)] for i in below}
        new_rows = {i: jnp.where(block, 0.0, rows[i]) for i in below}
        for p in range(PIVOT):
            d = a[p][0]
            for m in range(p):
                d = d - low[p][m] * low[p][m]
            y = lax.rsqrt(d)
            inv.append(y * (1.5 - (0.5 * d * y) * y))
            t, f = rt[p], r[p]
            for m in range(p):
                t = t - low[p][m] * scaled[m]
                f = f - low[p][m] * factor[m]
            scaled.append(t * inv[p])
            factor.append(f * inv[p])
            for i in below:
                t = column[i][p]
                for m in range(p):
                    t = t - low[p][m] * column[i][m]
                column[i][p] = t * inv[p]
                new_rows[i] = new_rows[i] - column[i][p] * scaled[p]
            for n in range(p + 1, PIVOT):
                t = a[p][n - p]
                for m in range(p):
                    t = t - low[n][m] * low[p][m]
                low[n][p] = t * inv[p]
        for i in range(vi, size // 8):
            new = new_rows.get(i, rows[i])
            if i == vi and i in new_rows:
                new = jnp.where(sub >= s + PIVOT, new, rows[i])
            if i == vi:
                up = upper[i] if s else jnp.zeros((8, size), F32)
                for p in range(PIVOT):
                    new = jnp.where((sub == s + p) & (lane <= k + p), scaled[p], new)
                    new = jnp.where((sub == s + p) & (lane > k + p), 0.0, new)
                    up = jnp.where((sub == s + p) & (lane >= k + p), factor[p], up)
                upper[i] = up
            rows[i] = new
    return jnp.concatenate(upper, axis=0), jnp.concatenate(rows, axis=0)


def orthonormalize(scale, gram, product, result, factor, weights):
    rank = gram.shape[0]

    @pl.when(pl.program_id(0) == 0)
    def _():
        upper, inverse = factorize(gram[...] * scale)
        factor[...] = upper
        turned = inverse.T
        high = turned.astype(BF16)
        low = (turned - high.astype(F32)).astype(BF16)
        both = jnp.concatenate([high, low], axis=1)
        weights[...] = jnp.concatenate([both, both], axis=0)

    for t in range(product.shape[0]):
        both = lax.dot_general(product[t], weights[...], (((0,), (0,)), ((), ())),
                               preferred_element_type=F32)
        result[t] = both[:, :rank] + both[:, rank:]


def per_device(rows_n, cols_n, blocks, block_slot, fetch_rows, basis):
    own, size, rank = basis.shape
    group = own * cols_n
    half = own // 2
    parts = half // PART
    per = cols_n * SLOTS
    span = group + 2 * HB
    vmem = pl.BlockSpec(memory_space=pltpu.VMEM)
    tile = (size, rank)
    dma = pltpu.SemaphoreType.DMA
    product, gram = pl.pallas_call(
        functools.partial(kernel, rows_n, cols_n),
        out_shape=(jax.ShapeDtypeStruct((own, 2 * rank, size), BF16),
                   jax.ShapeDtypeStruct((rank, rank), F32)),
        in_specs=[pl.BlockSpec(memory_space=pltpu.SMEM), vmem, vmem, pl.BlockSpec(memory_space=pl.ANY)],
        out_specs=(vmem, vmem),
        scratch_shapes=[
            pltpu.VMEM((rows_n, SLOTS, rows_n * cols_n), jnp.int32),
            pltpu.SMEM((rows_n, SLOTS, rows_n * cols_n), jnp.int32),
            pltpu.SMEM((2, group), jnp.int32),
            pltpu.VMEM((own,) + tile, BF16),
            pltpu.VMEM((own,) + tile, BF16),
            pltpu.VMEM((own,) + tile, BF16),
            pltpu.VMEM((own,) + tile, BF16),
            pltpu.VMEM((span,) + tile, BF16),
            [pltpu.VMEM((rows_n * per, w, size), BF16) for _, w in CHUNKS],
            [pltpu.VMEM((rows_n * per, w, size), BF16) for _, w in CHUNKS],
            pltpu.VMEM((2, 16, BAND, size, size), BF16),
            pltpu.VMEM((group, 2, size, size), BF16),
            pltpu.VMEM((group,) + tile, F32),
            pltpu.VMEM((own,) + tile, F32),
            [pltpu.VMEM((6, half, w, size), jnp.int16) for _, w in CHUNKS],
            pltpu.VMEM((N_CHUNKS, 6, parts, PART, size), F32),
            [pltpu.VMEM((6, half, w, size), jnp.int16) for _, w in CHUNKS],
            pltpu.VMEM((N_CHUNKS, 6, parts, PART, size), F32),
            pltpu.VMEM((8, rank // 8, rank), F32),
            pltpu.VMEM((8, rank // 8, rank), F32),
            pltpu.VMEM((rows_n // 2, rank // 8, rank), F32),
            pltpu.VMEM((8, rank // 8, rank), F32),
            dma((3,)),
            dma((4,)),
            dma((4,)),
            dma((4,)),
            dma((3,)),
            dma((2, rows_n)),
            dma((N_CHUNKS,)),
            dma((N_CHUNKS, 6, parts)),
            dma((N_CHUNKS, 6, parts)),
            dma((N_CHUNKS, 6, parts)),
            dma((N_CHUNKS, 6, parts)),
            dma((6,)),
            dma((4,)),
        ],
        compiler_params=pltpu.CompilerParams(
            collective_id=0, has_side_effects=True, vmem_limit_bytes=62 * 2**20),
        name="product_and_gram",
    )(block_slot.T, fetch_rows[0].T, basis, blocks)
    total_rows = rows_n * group * size
    steps = 2
    at_once = own // steps
    return tuple(pl.pallas_call(
        functools.partial(orthonormalize, 1.0 / total_rows),
        out_shape=(jax.ShapeDtypeStruct((own,) + tile, F32),
                   jax.ShapeDtypeStruct((rank, rank), F32)),
        grid=(steps,),
        in_specs=[pl.BlockSpec((rank, rank), lambda n: (0, 0)),
                  pl.BlockSpec((at_once, 2 * rank, size), lambda n: (n, 0, 0))],
        out_specs=(pl.BlockSpec((at_once,) + tile, lambda n: (n, 0, 0)),
                   pl.BlockSpec((rank, rank), lambda n: (0, 0))),
        scratch_shapes=[pltpu.VMEM((2 * rank, 2 * rank), BF16)],
        name="orthonormalize",
    )(gram, product))


def solution(mesh):
    in_specs = (
        P("rows", "col", None, None),
        P("rows", "col"),
        P(("rows", "col"), None, None),
        P(("rows", "col"), None, None),
    )
    out_specs = (P(("rows", "col"), None, None), P())
    step = functools.partial(per_device, mesh.shape["rows"], mesh.shape["col"])
    return jax.shard_map(
        step, mesh=mesh, in_specs=in_specs, out_specs=out_specs, check_vma=False
    )
```
